32 devices in a mesh: dp: 4 (over z), expert: 4 (over y, core), tensor: 2 (over x).
Axes of the slice: x: 2, y: 2, z: 4, core: 2. Of those that a mesh axis runs over, the one named last changes fastest.
Arguments:
- grad_out: bfloat16 [2048, 4096], P(('dp', 'expert'), 'tensor'), may hold values from -2 to 2
- route_ids: int32 [2048, 2], P(('dp', 'expert')), may hold values from 0 to 3, all different within a row; in each aligned block of 128 rows (0 to 127, 128 to 255, ...) at most 80 rows name the same one
- route_probs: bfloat16 [2048, 2], P(('dp', 'expert')), may hold values from 0.19921875 to 1
- saved_pre: bfloat16 [4, 4, 320, 1536], P('dp', 'expert'), may hold values from -6 to 6
- w_gate: bfloat16 [4, 4096, 768], P('expert', 'tensor'), may hold values from -0.21875 to 0.21875
- w_up: bfloat16 [4, 4096, 768], P('expert', 'tensor'), may hold values from -0.21875 to 0.21875
- w_down: bfloat16 [4, 768, 4096], P('expert', None, 'tensor'), may hold values from -0.09375 to 0.09375
Outputs:
- token_grad: bfloat16 [2048, 4096], P(('dp', 'expert'), 'tensor')
- prob_grad: bfloat16 [2048, 2], P(('dp', 'expert'))
- grad_down: bfloat16 [4, 768, 4096], P('expert', 'dp', 'tensor')
The draws below stay inside these ranges and needn't reach their ends.
Inputs may be any that keep to these rules, and one draw needn't show every extreme that they name: `route_ids`: each row names 2 different experts. In each aligned block of 128 rows (the tokens of one device) no expert is named by more than 80 rows, a bound that some block reaches.
All inputs are finite; a program needn't handle non-finite values.
Results may differ from the reference program's by a relative error of at most 0.015.
Values may be sent and summed in bfloat16 or wider, within the bound.
A program may use at most 64 MiB of HBM per device.

```python
import math
import jax
import jax.numpy as jnp
import numpy as np
from jax import lax

D = 4096
H = 768
TOPK = 2
TOK_DEV = 128
EXPERTS = 4
CAP = 80
TOKENS = 2048
N_DP = 4
N_EXPERT = 4


def steps_of(rng, extent, split, low, largest):
    loudness, own = 1.0, jax.random.fold_in(rng, 6)
    for dim, blocks in split:
        draws = jnp.exp(jax.random.uniform(jax.random.fold_in(own, dim), (blocks,), jnp.float32, low / len(split), largest / len(split)))
        loudness = loudness * jnp.repeat(draws, extent[dim] // blocks).reshape([-1 if axis == dim else 1 for axis in range(len(extent))])
    return loudness


def shared_out(stream_key, own, number, rows, number_of, top, limit, slope):
    sequence = jax.random.permutation(stream_key, number_of)
    heavy_load, usual = shares(number_of, rows * top, limit, slope, True), shares(number_of, rows * top, limit, slope, False)
    places = jnp.arange(number_of)

    def named(sizes, rotation):
        used = int((sizes > 0).sum())
        fixed = max(1, used // 4)
        shifted = fixed + (places - fixed + rotation * (used - fixed)) % max(1, number_of - fixed)
        return jnp.zeros((number_of,), jnp.int32).at[sequence[jnp.where(places < fixed, places, shifted)]].set(jnp.asarray(sizes, jnp.int32))

    sizes = jnp.where(number % 4 == 0, named(heavy_load, number // 4), named(usual, number - number // 4 - 1))
    mixed = jax.random.permutation(jax.random.fold_in(own, 3), number_of)
    source_of, receiver = mixed[0:number_of // 2 * 2:2], mixed[1:number_of // 2 * 2:2]
    room = jnp.minimum(sizes[source_of] - 1, limit - sizes[receiver]) // 2
    room = jnp.where((source_of == sequence[0]) | (receiver == sequence[0]) | (sizes[receiver] == 0), 0, jnp.maximum(room, 0))
    shifted = jax.random.randint(jax.random.fold_in(own, 4), (number_of // 2,), 0, 1 << 20) % (room + 1)
    sizes = sizes.at[source_of].add(-shifted).at[receiver].add(shifted)
    labels = jnp.searchsorted(jnp.cumsum(sizes), jnp.arange(rows * top), side="right").astype(jnp.int32)
    grid = labels.reshape(top, rows).T
    grid = grid[jax.random.permutation(jax.random.fold_in(own, 1), rows)]
    rotation = jax.random.randint(jax.random.fold_in(own, 2), (rows, 1), 0, top)
    return jnp.take_along_axis(grid, (jnp.arange(top)[None, :] + rotation) % top, axis=1)


def shares(number_of, total, most, lean, full):
    portions = [(1 << 20) // math.isqrt(rank ** lean) + 1 for rank in range(1, number_of + 1)]
    largest = most if full else min(most, max(-(-total // number_of), total * portions[0] // sum(portions)))
    least = 1 if total - largest >= number_of - 1 else 0
    holding, rest = [largest] + [least] * (number_of - 1), total - largest - least * (number_of - 1)
    while rest > 0:
        movable = [i for i in range(1, number_of) if holding[i] < largest] or [i for i in range(1, number_of) if holding[i] < most]
        mass, budget = sum([portions[i] for i in movable]), rest
        for i in movable:
            more = min(most - holding[i], max(1, budget * portions[i] // mass), rest)
            holding[i] = holding[i] + more
            rest = rest - more
    return np.array(holding)


def normal_values(key, dims, spread, limit, pieces=(), held_as=jnp.bfloat16):
    gain = steps_of(key, dims, pieces, -0.22, 0.18) if pieces else 1.0
    array = jax.random.normal(key, dims, jnp.float32) * spread * gain
    return jnp.minimum(jnp.maximum(array, -limit), limit).astype(held_as)


def setup_inputs(seed: int = 0) -> dict:
    key_of = jax.random.split(jax.random.key(seed), 8)
    grad_out = normal_values(key_of[0], (TOKENS, D), 0.3, 2.0, ((0, 16), (1, 2)))
    route_ids_keys = jax.random.split(jax.random.fold_in(key_of[1], 1), TOKENS // TOK_DEV)
    route_ids_turns = jax.random.permutation(jax.random.fold_in(key_of[1], 3), TOKENS // TOK_DEV)
    route_ids = jax.vmap(lambda own, number: shared_out(jax.random.fold_in(key_of[1], 2), own, number, TOK_DEV, EXPERTS, TOPK, CAP, 1))(route_ids_keys, route_ids_turns).reshape((TOKENS, TOPK))
    route_probs = jnp.clip(0.19921875 + 0.80078125 * jax.random.uniform(key_of[2], (TOKENS, TOPK), jnp.float32) ** steps_of(key_of[2], (TOKENS, TOPK), ((0, 16),), -0.2, 0.2), 0.19921875, 1.0).astype(jnp.bfloat16)
    saved_pre = normal_values(key_of[3], (N_DP, EXPERTS, N_EXPERT * CAP, 2 * H), 1.0, 6.0, ((0, 4), (1, 4)))
    w_gate = normal_values(key_of[4], (EXPERTS, D, H), H ** -0.5, 0.21875, ((0, 4), (1, 2)))
    w_up = normal_values(key_of[5], (EXPERTS, D, H), H ** -0.5, 0.21875, ((0, 4), (1, 2)))
    w_down = normal_values(key_of[6], (EXPERTS, H, D), D ** -0.5, 0.09375, ((0, 4), (2, 2)))
    return {"grad_out": grad_out, "route_ids": route_ids, "route_probs": route_probs, "saved_pre": saved_pre, "w_gate": w_gate, "w_up": w_up, "w_down": w_down}


def slot_index(id_block):
    flat = id_block.reshape(-1).astype(jnp.int32)
    onehot = (flat[:, None] == jnp.arange(EXPERTS, dtype=jnp.int32)[None, :]).astype(jnp.int32)
    before = jnp.cumsum(onehot, axis=0) - onehot
    position = jnp.sum(before * onehot, axis=1).astype(jnp.int32)
    return (flat * CAP + position).astype(jnp.int32)


def dispatch(dy_block, id_block, prob_block):
    slots = slot_index(id_block)
    source = jnp.zeros((EXPERTS * CAP,), jnp.int32).at[slots].set(jnp.arange(TOK_DEV * TOPK, dtype=jnp.int32) + 1)
    valid = source > 0
    flat_src = jnp.maximum(source - 1, 0).astype(jnp.int32)
    rows = jnp.where(valid[:, None], dy_block[flat_src // TOPK], jnp.zeros((), dy_block.dtype))
    probs = jnp.where(valid, prob_block.reshape(-1)[flat_src], jnp.zeros((), prob_block.dtype))
    return rows.reshape(EXPERTS, CAP, D), probs.reshape(EXPERTS, CAP)


def expert_step(operands):
    pre, wgate, wup, wdown, dyr, prob = operands
    gate = pre[:, :H].astype(jnp.float32)
    upper = pre[:, H:].astype(jnp.float32)
    sig = jax.nn.sigmoid(gate)
    act = gate * sig
    hid = act * upper
    p32 = prob.astype(jnp.float32)[:, None]
    dh = jnp.dot(dyr, wdown.T, preferred_element_type=jnp.float32)
    route = jnp.sum(dh * hid, axis=1).astype(jnp.bfloat16)
    scaled = p32 * dh
    dgate = (scaled * upper * sig * (1.0 + gate * (1.0 - sig))).astype(jnp.bfloat16)
    dup = (scaled * act).astype(jnp.bfloat16)
    hpro = (p32 * hid).astype(jnp.bfloat16)
    dx = jnp.dot(dgate, wgate.T, preferred_element_type=jnp.float32) + jnp.dot(dup, wup.T, preferred_element_type=jnp.float32)
    part = jnp.dot(hpro.T, dyr, preferred_element_type=jnp.float32).astype(jnp.bfloat16)
    return dx.astype(jnp.bfloat16), route, part


def collect(flat_rows, flat_route, id_block):
    slots = slot_index(id_block)
    picked = flat_rows[slots].astype(jnp.float32).reshape(TOK_DEV, TOPK, D)
    return jnp.sum(picked, axis=1).astype(jnp.bfloat16), flat_route[slots].reshape(TOK_DEV, TOPK)


def replica(operands):
    dy_group, id_group, prob_group, pre_group, w_gate, w_up, w_down = operands
    rows, probs = jax.vmap(dispatch)(dy_group, id_group, prob_group)
    rows = rows.transpose(1, 0, 2, 3).reshape(EXPERTS, N_EXPERT * CAP, D)
    probs = probs.transpose(1, 0, 2).reshape(EXPERTS, N_EXPERT * CAP)
    dx, route, part = lax.map(expert_step, (pre_group, w_gate, w_up, w_down, rows, probs))
    back = dx.reshape(EXPERTS, N_EXPERT, CAP, D).transpose(1, 0, 2, 3).reshape(N_EXPERT, EXPERTS * CAP, D)
    rback = route.reshape(EXPERTS, N_EXPERT, CAP).transpose(1, 0, 2).reshape(N_EXPERT, EXPERTS * CAP)
    tok, pgrad = jax.vmap(collect)(back, rback, id_group)
    return tok, pgrad, part


def reference(grad_out, route_ids, route_probs, saved_pre, w_gate, w_up, w_down):
    dy4 = grad_out.reshape(N_DP, N_EXPERT, TOK_DEV, D)
    ids4 = route_ids.reshape(N_DP, N_EXPERT, TOK_DEV, TOPK)
    pr4 = route_probs.reshape(N_DP, N_EXPERT, TOK_DEV, TOPK)
    outputs = []
    for replica_index in range(N_DP):
        outputs.append(replica((dy4[replica_index], ids4[replica_index], pr4[replica_index], saved_pre[replica_index], w_gate, w_up, w_down)))
    token_grad = jnp.stack([item[0] for item in outputs]).reshape(TOKENS, D)
    prob_grad = jnp.stack([item[1] for item in outputs]).reshape(TOKENS, TOPK)
    parts = lax.optimization_barrier(jnp.stack([item[2] for item in outputs]))
    grad_down = jnp.sum(parts.astype(jnp.float32), axis=0).astype(jnp.bfloat16)
    return token_grad, prob_grad, grad_down
```

```python
import functools

import jax
import jax.numpy as jnp
from jax import lax
from jax.experimental import pallas as pl
from jax.experimental.pallas import tpu as pltpu
from jax.sharding import PartitionSpec as P

MESH = pl.DeviceIdType.MESH
BF16, F32 = jnp.bfloat16, jnp.float32
LANES = 128


def dot(a, b, ca=1, cb=0):
    return lax.dot_general(a, b, (((ca,), (cb,)), ((), ())), preferred_element_type=F32)


def fused(
    n_z, cap, nb,
    ids_ref, prob_ref, tok_hbm, pre_hbm, wg_hbm, wu_hbm, wd_hbm,
    tg_ref, pg_ref, gd_ref,
    tok, pre, wg, wu, wd,
    onehot_t, meta_s, meta_r, rows_s, disp,
    slope, act_v, hid_v, hp, hp_t,
    dh, dh_s, dh_r, dg, du, dx, back, rt_s, rt_r,
    up_s, up_r, lo_s, lo_r,
    tok_sem, pre_sem, w_sem,
    meta_ss, meta_rs, disp_ss, disp_rs, dh_ss, dh_rs, back_ss, back_rs, rt_ss, rt_rs,
    up_ss, up_rs, lo_ss, lo_rs,
):
    z, me, x = lax.axis_index("dp"), lax.axis_index("expert"), lax.axis_index("tensor")
    peer = [me, me + 1 - 2 * (me % 2), (me + 2) % 4, 3 - me]
    far = (2, 3, 1)
    tokens, width = tok.shape[0], tok.shape[1]
    bw = width // nb
    hidden = wd.shape[0]
    piece = hidden // n_z

    def rows(k):
        return pl.ds(k * cap, cap)

    def cols(j):
        return pl.ds(j * bw, bw)

    def to_peer(src, dst, ss, rs, k):
        return pltpu.make_async_remote_copy(src, dst, ss, rs, device_id={"expert": peer[k]}, device_id_type=MESH)

    def meta_copy(k):
        return to_peer(meta_s.at[rows(k)], meta_r.at[rows(k)], meta_ss.at[k], meta_rs.at[k], k)

    def disp_copy(k, j):
        return to_peer(rows_s.at[j, rows(k)], disp.at[j, rows(k)], disp_ss.at[k, j], disp_rs.at[k, j], k)

    def back_copy(k, j):
        return to_peer(dx.at[j, rows(k)], back.at[j, rows(k)], back_ss.at[k, j], back_rs.at[k, j], k)

    def rt_copy(k):
        return to_peer(rt_s.at[rows(k)], rt_r.at[rows(k)], rt_ss.at[k], rt_rs.at[k], k)

    def dh_copy(k):
        return pltpu.make_async_remote_copy(
            dh_s.at[rows(k)], dh_r.at[rows(k)], dh_ss.at[k], dh_rs.at[k],
            device_id={"tensor": 1 - x}, device_id_type=MESH)

    def up_copy(d, j):
        return pltpu.make_async_remote_copy(
            up_s.at[d, j], up_r.at[d, j], up_ss.at[d, j], up_rs.at[d, j],
            device_id={"dp": z + 1}, device_id_type=MESH)

    def lo_copy(d, j):
        return pltpu.make_async_remote_copy(
            lo_s.at[d, j], lo_r.at[d, j], lo_ss.at[d, j], lo_rs.at[d, j],
            device_id={"dp": z - 1}, device_id_type=MESH)

    tok_in = [pltpu.make_async_copy(tok_hbm.at[:, cols(j)], tok.at[:, cols(j)], tok_sem.at[j]) for j in range(nb)]
    pre_in = [
        pltpu.make_async_copy(pre_hbm.at[pl.ds(pl.multiple_of(peer[k] * cap, 16), cap)], pre.at[rows(k)], pre_sem.at[k])
        for k in range(4)
    ]
    w_in = [
        pltpu.make_async_copy(wd_hbm, wd, w_sem.at[0]),
        pltpu.make_async_copy(wg_hbm, wg, w_sem.at[1]),
        pltpu.make_async_copy(wu_hbm, wu, w_sem.at[2]),
    ]
    for c in tok_in + pre_in + w_in:
        c.start()

    barrier = pltpu.get_barrier_semaphore()
    for k in (1, 2, 3):
        pl.semaphore_signal(barrier, inc=1, device_id={"expert": peer[k]}, device_id_type=MESH)
    pl.semaphore_signal(barrier, inc=1, device_id={"tensor": 1 - x}, device_id_type=MESH)

    @pl.when(z > 0)
    def _():
        pl.semaphore_signal(barrier, inc=1, device_id={"dp": z - 1}, device_id_type=MESH)

    @pl.when(z < n_z - 1)
    def _():
        pl.semaphore_signal(barrier, inc=1, device_id={"dp": z + 1}, device_id_type=MESH)

    ids = ids_ref[...]
    prb = prob_ref[...].astype(F32)
    lane = lax.broadcasted_iota(jnp.int32, (tokens, LANES), 1)
    row_i = lax.broadcasted_iota(jnp.int32, (tokens, tokens), 0)
    col_i = lax.broadcasted_iota(jnp.int32, (tokens, tokens), 1)
    lower = (col_i < row_i).astype(F32).astype(BF16)
    first, second = ids[:, 0:1], ids[:, 1:2]
    pick = []
    for k in range(4):
        m = ((first == peer[k]) | (second == peer[k])).astype(F32)
        mb = jnp.broadcast_to(m, (tokens, LANES))
        pos = dot(lower, mb.astype(BF16))
        sel = jnp.where(pos == lane.astype(F32), mb, 0.0)
        onehot_t[k] = sel.astype(BF16)
        s = sel.T[:cap].astype(BF16)
        pick.append(s)
        pk = jnp.where(first == peer[k], prb[:, 0:1], jnp.where(second == peer[k], prb[:, 1:2], 0.0))
        meta = dot(s, jnp.broadcast_to(pk, (tokens, LANES)).astype(BF16)).astype(BF16)
        if k == 0:
            meta_r[rows(0)] = meta
        else:
            meta_s[rows(k)] = meta

    @pl.when((z > 0) & (z < n_z - 1))
    def _():
        pl.semaphore_wait(barrier, 6)

    @pl.when((z == 0) | (z == n_z - 1))
    def _():
        pl.semaphore_wait(barrier, 5)

    for k in far:
        meta_copy(k).start()
    for j in range(nb):
        tok_in[j].wait()
        block = tok[:, cols(j)]
        for k in far:
            rows_s[j, rows(k)] = dot(pick[k], block).astype(BF16)
            disp_copy(k, j).start()
        disp[j, rows(0)] = dot(pick[0], block).astype(BF16)

    for k in range(4):
        pre_in[k].wait()
        if k:
            meta_copy(k).wait_recv()
        p = meta_r[rows(k)].astype(F32)[:, 0:1]
        g = pre[rows(k), :hidden].astype(F32)
        u = pre[rows(k), hidden:].astype(F32)
        sg = jax.nn.sigmoid(g)
        act = g * sg
        hid = act * u
        act_v[rows(k)] = act
        hid_v[rows(k)] = hid
        slope[rows(k)] = u * sg * (1.0 + g * (1.0 - sg))
        hp[rows(k)] = p * hid
    for h in range(0, hidden, LANES):
        hp_t[pl.ds(h, LANES)] = hp[:, pl.ds(h, LANES)].T.astype(BF16)

    def product(d, j):
        return dot(hp_t[pl.ds(pl.multiple_of(d * piece, 16), piece)], disp[j])

    def send_up(d, j, inner):
        v = product(d, j)
        if inner:
            up_copy(d, j).wait_recv()
            v = v + up_r[d, j].astype(F32)
        up_s[d, j] = v.astype(BF16)
        up_copy(d, j).start()

    def send_lo(d, j, inner):
        v = product(d, j)
        if inner:
            lo_copy(d, j).wait_recv()
            v = v + lo_r[d, j].astype(F32)
        lo_s[d, j] = v.astype(BF16)
        lo_copy(d, j).start()

    w_in[0].wait()
    for j in range(nb):
        for k in far:
            disp_copy(k, j).wait_recv()

        @pl.when(z == 0)
        def _():
            send_up(n_z - 1, j, False)

        @pl.when(z == n_z - 1)
        def _():
            send_lo(0, j, False)

        part = dot(disp[j], wd[:, cols(j)], 1, 1)
        if j == 0:
            dh[...] = part
        elif j < nb - 1:
            dh[...] += part
        else:
            part = (dh[...] + part).astype(BF16)
            dh_s[...] = part
    for k in (2, 3, 1, 0):
        dh_copy(k).start()

    @pl.when(z == 0)
    def _():
        for d in range(n_z - 2, 0, -1):
            for j in range(nb):
                send_up(d, j, False)

    @pl.when(z == n_z - 1)
    def _():
        for d in range(1, n_z - 1):
            for j in range(nb):
                send_lo(d, j, False)

    def inner_step(t, blocks):
        for j in blocks:
            @pl.when((z > 0) & (z < n_z - 1 - t))
            def _():
                send_up(n_z - 1 - t, j, True)

            @pl.when((z < n_z - 1) & (z > t))
            def _():
                send_lo(t, j, True)

    def input_grad(pair):
        lo = min(pair) * cap
        for k in pair:
            dh_copy(k).wait_recv()
            d = dh_s[rows(k)].astype(F32) + dh_r[rows(k)].astype(F32)
            route = jnp.sum(d * hid_v[rows(k)], axis=1, keepdims=True)
            route = jnp.broadcast_to(route, (cap, LANES)).astype(BF16)
            a = meta_r[rows(k)].astype(F32)[:, 0:1] * d
            dg[rows(k)] = (a * slope[rows(k)]).astype(BF16)
            du[rows(k)] = (a * act_v[rows(k)]).astype(BF16)
            if k:
                rt_s[rows(k)] = route
                rt_copy(k).start()
            else:
                rt_r[rows(0)] = route
        both = pl.ds(lo, 2 * cap)
        for j in range(nb):
            v = dot(dg[both], wg[cols(j)], 1, 1) + dot(du[both], wu[cols(j)], 1, 1)
            v = v.astype(BF16)
            dx[j, both] = v
            for k in pair:
                if k:
                    back_copy(k, j).start()

    inner_step(0, range(0, nb // 2))
    w_in[1].wait()
    w_in[2].wait()
    input_grad((2, 3))
    inner_step(0, range(nb // 2, nb))
    input_grad((1, 0))
    for t in range(1, n_z - 1):
        inner_step(t, range(nb))

    for j in range(nb):
        v = dot(onehot_t[0, :, :cap], dx[j, rows(0)])
        for k in (1, 2, 3):
            back_copy(k, j).wait_recv()
            v = v + dot(onehot_t[k, :, :cap], back[j, rows(k)])
        tg_ref[:, cols(j)] = v.astype(BF16)
    v0 = jnp.zeros((tokens, LANES), F32)
    v1 = jnp.zeros((tokens, LANES), F32)
    for k in range(4):
        if k:
            rt_copy(k).wait_recv()
        r = dot(onehot_t[k, :, :cap], rt_r[rows(k)])
        v0 = v0 + jnp.where(first == peer[k], r, 0.0)
        v1 = v1 + jnp.where(second == peer[k], r, 0.0)
    pg_ref[...] = jnp.where(lane == 0, v0, v1)[:, :2].astype(BF16)

    own = z
    for j in range(nb):
        hold = dh.at[pl.ds(0, piece), pl.ds(0, bw)]
        hold[...] = product(own, j)

        @pl.when(z > 0)
        def _():
            up_copy(own, j).wait_recv()
            hold[...] += up_r[own, j].astype(F32)

        @pl.when(z < n_z - 1)
        def _():
            lo_copy(own, j).wait_recv()
            hold[...] += lo_r[own, j].astype(F32)

        gd_ref[:, cols(j)] = hold[...].astype(BF16)

    for k in (1, 2, 3):
        meta_copy(k).wait_send()
        rt_copy(k).wait_send()
        for j in range(nb):
            disp_copy(k, j).wait_send()
            back_copy(k, j).wait_send()
    for k in range(4):
        dh_copy(k).wait_send()
    for d in range(n_z):
        for j in range(nb):
            @pl.when(z < d)
            def _():
                up_copy(d, j).wait_send()

            @pl.when(z > d)
            def _():
                lo_copy(d, j).wait_send()


def fused_shards(n_z, grad_out, route_ids, route_probs, saved_pre, w_gate, w_up, w_down):
    tok, width = grad_out.shape
    slot_rows = saved_pre.shape[2]
    cap = slot_rows // 4
    hidden = saved_pre.shape[3] // 2
    nb = 4
    bw = width // nb
    piece = hidden // n_z
    vmem = pl.BlockSpec(memory_space=pltpu.VMEM)
    hbm = pl.BlockSpec(memory_space=pl.ANY)
    dma = pltpu.SemaphoreType.DMA
    blocks = (nb, slot_rows, bw)
    hops = (n_z, nb, piece, bw)
    return pl.pallas_call(
        functools.partial(fused, n_z, cap, nb),
        out_shape=(
            jax.ShapeDtypeStruct((tok, width), BF16),
            jax.ShapeDtypeStruct(route_probs.shape, BF16),
            jax.ShapeDtypeStruct((piece, width), BF16),
        ),
        in_specs=[vmem, vmem, hbm, hbm, hbm, hbm, hbm],
        out_specs=(vmem, vmem, vmem),
        scratch_shapes=[
            pltpu.VMEM((tok, width), BF16),
            pltpu.VMEM((slot_rows, 2 * hidden), BF16),
            pltpu.VMEM((width, hidden), BF16),
            pltpu.VMEM((width, hidden), BF16),
            pltpu.VMEM((hidden, width), BF16),
            pltpu.VMEM((4, tok, LANES), BF16),
            pltpu.VMEM((slot_rows, LANES), BF16),
            pltpu.VMEM((slot_rows, LANES), BF16),
            pltpu.VMEM(blocks, BF16),
            pltpu.VMEM(blocks, BF16),
            pltpu.VMEM((slot_rows, hidden), F32),
            pltpu.VMEM((slot_rows, hidden), F32),
            pltpu.VMEM((slot_rows, hidden), F32),
            pltpu.VMEM((slot_rows, hidden), F32),
            pltpu.VMEM((hidden, slot_rows), BF16),
            pltpu.VMEM((slot_rows, hidden), F32),
            pltpu.VMEM((slot_rows, hidden), BF16),
            pltpu.VMEM((slot_rows, hidden), BF16),
            pltpu.VMEM((slot_rows, hidden), BF16),
            pltpu.VMEM((slot_rows, hidden), BF16),
            pltpu.VMEM(blocks, BF16),
            pltpu.VMEM(blocks, BF16),
            pltpu.VMEM((slot_rows, LANES), BF16),
            pltpu.VMEM((slot_rows, LANES), BF16),
            pltpu.VMEM(hops, BF16),
            pltpu.VMEM(hops, BF16),
            pltpu.VMEM(hops, BF16),
            pltpu.VMEM(hops, BF16),
            dma((nb,)), dma((4,)), dma((3,)),
            dma((4,)), dma((4,)), dma((4, nb)), dma((4, nb)), dma((4,)), dma((4,)),
            dma((4, nb)), dma((4, nb)), dma((4,)), dma((4,)),
            dma((n_z, nb)), dma((n_z, nb)), dma((n_z, nb)), dma((n_z, nb)),
        ],
        compiler_params=pltpu.CompilerParams(
            collective_id=0, has_side_effects=True, vmem_limit_bytes=56 * 1024 * 1024
        ),
    )(route_ids, route_probs, grad_out, saved_pre[0, 0], w_gate[0], w_up[0], w_down[0])


def takes_fused(shape, width, hidden, capacity):
    return (
        shape["expert"] == 4 and shape["tensor"] == 2 and shape["dp"] > 1 and capacity % 16 == 0 and capacity <= LANES
        and width % (4 * LANES) == 0 and hidden % LANES == 0 and (hidden // shape["dp"]) % 16 == 0
    )


def slot_index(id_block, n_experts, capacity):
    flat = id_block.reshape(-1)
    onehot = (flat[:, None] == jnp.arange(n_experts, dtype=jnp.int32)[None, :]).astype(jnp.int32)
    before = jnp.cumsum(onehot, axis=0) - onehot
    position = jnp.sum(before * onehot, axis=1)
    return flat * capacity + position


def backward_rows(dh_rows, gate, upper, sig, act, hid, p32):
    route = jnp.sum(dh_rows * hid, axis=1).astype(jnp.bfloat16)
    scaled = p32 * dh_rows
    dgate = (scaled * upper * sig * (1.0 + gate * (1.0 - sig))).astype(jnp.bfloat16)
    dup = (scaled * act).astype(jnp.bfloat16)
    return (dgate, dup, route)


def shards(grad_out, route_ids, route_probs, saved_pre, w_gate, w_up, w_down):
    n_exp = lax.axis_size("expert")
    slot_rows = saved_pre.shape[2]
    capacity = slot_rows // n_exp
    tok = grad_out.shape[0]
    topk = route_ids.shape[1]
    width = grad_out.shape[1]
    hidden = saved_pre.shape[3] // 2
    slots = slot_index(route_ids, n_exp, capacity)
    source = (
        jnp.zeros((n_exp * capacity,), jnp.int32)
        .at[slots]
        .set(jnp.arange(tok * topk, dtype=jnp.int32) + 1)
    )
    valid = source > 0
    flat_src = jnp.maximum(source - 1, 0)
    send_rows = jnp.where(valid[:, None], grad_out[flat_src // topk], jnp.zeros((), jnp.bfloat16))
    send_prob = jnp.where(valid, route_probs.reshape(-1)[flat_src], jnp.zeros((), jnp.bfloat16))
    got_rows, got_prob = (
        lax.all_to_all(
            send_rows.reshape(n_exp, capacity, width),
            "expert",
            split_axis=0,
            concat_axis=0,
            tiled=True,
        ),
        lax.all_to_all(
            send_prob.reshape(n_exp, capacity), "expert", split_axis=0, concat_axis=0, tiled=True
        ),
    )
    dyr = got_rows.reshape(slot_rows, width)
    p32 = got_prob.reshape(slot_rows, 1).astype(jnp.float32)
    pre = saved_pre[0, 0]
    gate = pre[:, :hidden].astype(jnp.float32)
    upper = pre[:, hidden:].astype(jnp.float32)
    sig = jax.nn.sigmoid(gate)
    act = gate * sig
    hid = act * upper
    hpro = (p32 * hid).astype(jnp.bfloat16)
    down_term = lax.dot_general(
        hpro, dyr, (((0,), (0,)), ((), ())), preferred_element_type=jnp.float32
    )
    dh_part = lax.dot_general(
        dyr, w_down[0], (((1,), (1,)), ((), ())), preferred_element_type=jnp.float32
    )
    dh_rows = lax.psum(dh_part.astype(jnp.bfloat16), "tensor").astype(jnp.float32)
    dgate, dup, route = backward_rows(dh_rows, gate, upper, sig, act, hid, p32)
    dx = lax.dot_general(
        dgate, w_gate[0], (((1,), (1,)), ((), ())), preferred_element_type=jnp.float32
    )
    dx = dx + lax.dot_general(
        dup, w_up[0], (((1,), (1,)), ((), ())), preferred_element_type=jnp.float32
    )
    dx = dx.astype(jnp.bfloat16)
    back_rows, back_route = (
        lax.all_to_all(
            dx.reshape(n_exp, capacity, width), "expert", split_axis=0, concat_axis=0, tiled=True
        ),
        lax.all_to_all(
            route.reshape(n_exp, capacity), "expert", split_axis=0, concat_axis=0, tiled=True
        ),
    )
    picked = back_rows.reshape(n_exp * capacity, width)[slots].reshape(tok, topk, width)
    token_grad = jnp.sum(picked.astype(jnp.float32), axis=1).astype(jnp.bfloat16)
    prob_grad = back_route.reshape(n_exp * capacity)[slots].reshape(tok, topk)
    grad_down = lax.psum_scatter(
        down_term[None].astype(jnp.bfloat16), "dp", scatter_dimension=1, tiled=True
    )
    return (token_grad, prob_grad, grad_down)


def solution(mesh):
    shape = dict(mesh.shape)

    def local(*args):
        saved_pre, w_down = args[3], args[6]
        capacity = saved_pre.shape[2] // shape["expert"]
        tok = args[0].shape[0]
        if tok == LANES and takes_fused(shape, w_down.shape[2], w_down.shape[1], capacity):
            return tuple(
                v[None] if i == 2 else v for i, v in enumerate(fused_shards(shape["dp"], *args))
            )
        return shards(*args)

    return jax.shard_map(
        local,
        mesh=mesh,
        in_specs=(
            P(("dp", "expert"), "tensor"),
            P(("dp", "expert"), None),
            P(("dp", "expert"), None),
            P("dp", "expert", None, None),
            P("expert", "tensor", None),
            P("expert", "tensor", None),
            P("expert", None, "tensor"),
        ),
        out_specs=(
            P(("dp", "expert"), "tensor"),
            P(("dp", "expert"), None),
            P("expert", "dp", "tensor"),
        ),
        check_vma=False,
    )
```

```python
import functools

import jax
import jax.numpy as jnp
from jax import lax
from jax.experimental import pallas as pl
from jax.experimental.pallas import tpu as pltpu
from jax.sharding import PartitionSpec as P

MESH = pl.DeviceIdType.MESH
BF16, F32 = jnp.bfloat16, jnp.float32
LANES = 128


def dot(a, b, ca=1, cb=0):
    return lax.dot_general(a, b, (((ca,), (cb,)), ((), ())), preferred_element_type=F32)


def fused(
    n_z, cap, nb,
    names_ref, tok_hbm, pre_hbm, wg_hbm, wu_hbm, wd_hbm,
    tg_ref, pg_ref, gd_ref,
    tok, pre, wg, wu, wd,
    onehot_t, meta_s, meta_r, rows_s, disp,
    slope, act_v, hid_v, hp, hp_t,
    dh, dh_s, dh_r, dg, du, dx, back, rt_s, rt_r,
    up_s, up_r, lo_s, lo_r, far_disp, far_hp,
    tok_sem, pre_sem, w_sem,
    meta_ss, meta_rs, disp_ss, disp_rs, dh_ss, dh_rs, back_ss, back_rs, rt_ss, rt_rs,
    up_ss, up_rs, lo_ss, lo_rs, end_ss, end_rs,
):
    z, me, x = lax.axis_index("dp"), lax.axis_index("expert"), lax.axis_index("tensor")
    peer = [me, me + 1 - 2 * (me % 2), (me + 2) % 4, 3 - me]
    far = (2, 3, 1)
    tokens, width = tok.shape[0], tok.shape[1]
    bw = width // nb
    hidden = wd.shape[0]
    piece = hidden // n_z

    def rows(k):
        return pl.ds(k * cap, cap)

    def cols(j):
        return pl.ds(j * bw, bw)

    def to_peer(src, dst, ss, rs, k):
        return pltpu.make_async_remote_copy(src, dst, ss, rs, device_id={"expert": peer[k]}, device_id_type=MESH)

    def meta_copy(k):
        return to_peer(meta_s.at[rows(k)], meta_r.at[rows(k)], meta_ss.at[k], meta_rs.at[k], k)

    def disp_copy(k, j):
        return to_peer(rows_s.at[j, rows(k)], disp.at[j, rows(k)], disp_ss.at[k, j], disp_rs.at[k, j], k)

    def back_copy(k, j):
        return to_peer(dx.at[j, rows(k)], back.at[j, rows(k)], back_ss.at[k, j], back_rs.at[k, j], k)

    def rt_copy(k):
        return to_peer(rt_s.at[rows(k)], rt_r.at[rows(k)], rt_ss.at[k], rt_rs.at[k], k)

    def dh_copy(k):
        return pltpu.make_async_remote_copy(
            dh_s.at[rows(k)], dh_r.at[rows(k)], dh_ss.at[k], dh_rs.at[k],
            device_id={"tensor": 1 - x}, device_id_type=MESH)

    def up_copy(d, j):
        return pltpu.make_async_remote_copy(
            up_s.at[d, j], up_r.at[d, j], up_ss.at[d, j], up_rs.at[d, j],
            device_id={"dp": z + 1}, device_id_type=MESH)

    def lo_copy(d, j):
        return pltpu.make_async_remote_copy(
            lo_s.at[d, j], lo_r.at[d, j], lo_ss.at[d, j], lo_rs.at[d, j],
            device_id={"dp": z - 1}, device_id_type=MESH)

    def end_copy(j, step):
        return pltpu.make_async_remote_copy(
            disp.at[j], far_disp.at[j], end_ss.at[j], end_rs.at[j],
            device_id={"dp": z + step}, device_id_type=MESH)

    def end_hp_copy(step):
        part = pl.ds(piece if step > 0 else 0, hidden - piece)
        return pltpu.make_async_remote_copy(
            hp_t.at[part], far_hp.at[part], end_ss.at[nb], end_rs.at[nb],
            device_id={"dp": z + step}, device_id_type=MESH)

    def at_ends(act):
        @pl.when(z == 0)
        def _():
            act(1)

        @pl.when(z == n_z - 1)
        def _():
            act(-1)

    tok_in = [pltpu.make_async_copy(tok_hbm.at[:, cols(j)], tok.at[:, cols(j)], tok_sem.at[j]) for j in range(nb)]
    pre_in = [
        pltpu.make_async_copy(pre_hbm.at[pl.ds(pl.multiple_of(peer[k] * cap, 16), cap)], pre.at[rows(k)], pre_sem.at[k])
        for k in range(4)
    ]
    w_in = [
        pltpu.make_async_copy(wd_hbm, wd, w_sem.at[0]),
        pltpu.make_async_copy(wg_hbm, wg, w_sem.at[1]),
        pltpu.make_async_copy(wu_hbm, wu, w_sem.at[2]),
    ]
    for c in tok_in + pre_in + w_in:
        c.start()

    barrier = pltpu.get_barrier_semaphore()
    for k in (1, 2, 3):
        pl.semaphore_signal(barrier, inc=1, device_id={"expert": peer[k]}, device_id_type=MESH)
    pl.semaphore_signal(barrier, inc=1, device_id={"tensor": 1 - x}, device_id_type=MESH)

    @pl.when(z > 0)
    def _():
        pl.semaphore_signal(barrier, inc=1, device_id={"dp": z - 1}, device_id_type=MESH)

    @pl.when(z < n_z - 1)
    def _():
        pl.semaphore_signal(barrier, inc=1, device_id={"dp": z + 1}, device_id_type=MESH)

    names = names_ref[...]
    ids, prb = names[:, 0:2].astype(jnp.int32), names[:, 2:4]
    lane = lax.broadcasted_iota(jnp.int32, (tokens, LANES), 1)
    row_i = lax.broadcasted_iota(jnp.int32, (tokens, tokens), 0)
    col_i = lax.broadcasted_iota(jnp.int32, (tokens, tokens), 1)
    lower = (col_i < row_i).astype(F32).astype(BF16)
    first, second = ids[:, 0:1], ids[:, 1:2]
    pick = []
    for k in range(4):
        m = ((first == peer[k]) | (second == peer[k])).astype(F32)
        mb = jnp.broadcast_to(m, (tokens, LANES))
        pos = dot(lower, mb.astype(BF16))
        sel = jnp.where(pos == lane.astype(F32), mb, 0.0)
        onehot_t[k] = sel.astype(BF16)
        s = sel.T[:cap].astype(BF16)
        pick.append(s)
        pk = jnp.where(first == peer[k], prb[:, 0:1], jnp.where(second == peer[k], prb[:, 1:2], 0.0))
        meta = dot(s, jnp.broadcast_to(pk, (tokens, LANES)).astype(BF16)).astype(BF16)
        if k == 0:
            meta_r[rows(0)] = meta
        else:
            meta_s[rows(k)] = meta

    @pl.when((z > 0) & (z < n_z - 1))
    def _():
        pl.semaphore_wait(barrier, 6)

    @pl.when((z == 0) | (z == n_z - 1))
    def _():
        pl.semaphore_wait(barrier, 5)

    for k in far:
        meta_copy(k).start()
    for j in range(nb):
        tok_in[j].wait()
        block = tok[:, cols(j)]
        for k in far:
            rows_s[j, rows(k)] = dot(pick[k], block).astype(BF16)
            disp_copy(k, j).start()
        disp[j, rows(0)] = dot(pick[0], block).astype(BF16)

    for k in range(4):
        pre_in[k].wait()
        if k:
            meta_copy(k).wait_recv()
        p = meta_r[rows(k)].astype(F32)[:, 0:1]
        g = pre[rows(k), :hidden].astype(F32)
        u = pre[rows(k), hidden:].astype(F32)
        sg = jax.nn.sigmoid(g)
        act = g * sg
        hid = act * u
        act_v[rows(k)] = act
        hid_v[rows(k)] = hid
        slope[rows(k)] = u * sg * (1.0 + g * (1.0 - sg))
        hp[rows(k)] = p * hid
    for h in range(0, hidden, LANES):
        hp_t[pl.ds(h, LANES)] = hp[:, pl.ds(h, LANES)].T.astype(BF16)

    def product(d, j):
        return dot(hp_t[pl.ds(pl.multiple_of(d * piece, 16), piece)], disp[j])

    def far_product(d, j):
        return dot(far_hp[pl.ds(pl.multiple_of(d * piece, 16), piece)], far_disp[j])

    def send_up(d, j, inner):
        v = product(d, j)
        if inner:
            up_copy(d, j).wait_recv()
            v = v + up_r[d, j].astype(F32)
        else:
            v = v + far_product(d, j)
        up_s[d, j] = v.astype(BF16)
        up_copy(d, j).start()

    def send_lo(d, j, inner):
        v = product(d, j)
        if inner:
            lo_copy(d, j).wait_recv()
            v = v + lo_r[d, j].astype(F32)
        else:
            v = v + far_product(d, j)
        lo_s[d, j] = v.astype(BF16)
        lo_copy(d, j).start()

    at_ends(lambda step: end_hp_copy(step).start())
    w_in[0].wait()
    for j in range(nb):
        for k in far:
            disp_copy(k, j).wait_recv()

        if j < 2:
            at_ends(lambda step: end_copy(j, step).start())
        part = dot(disp[j], wd[:, cols(j)], 1, 1)
        if j == 0:
            dh[...] = part
        elif j < nb - 1:
            dh[...] += part
        else:
            part = (dh[...] + part).astype(BF16)
            dh_s[...] = part
    for k in (2, 3, 1, 0):
        dh_copy(k).start()

    def end_next(j):
        def go(step):
            end_copy(j - 2, step).wait_send()
            end_copy(j, step).start()

        at_ends(go)

    def far_step(j):
        @pl.when(z == 1)
        def _():
            if j == 0:
                end_hp_copy(1).wait_recv()
            end_copy(j, 1).wait_recv()
            for d in range(n_z - 1, 1, -1):
                send_up(d, j, False)

        @pl.when(z == n_z - 2)
        def _():
            if j == 0:
                end_hp_copy(-1).wait_recv()
            end_copy(j, -1).wait_recv()
            for d in range(n_z - 2):
                send_lo(d, j, False)

    def inner_step(j):
        for t in range(n_z - 3):
            @pl.when((z > 1) & (z < n_z - 1 - t))
            def _():
                send_up(n_z - 1 - t, j, True)

            @pl.when((z < n_z - 2) & (z > t))
            def _():
                send_lo(t, j, True)

    def input_grad(pair):
        lo = min(pair) * cap
        for k in pair:
            dh_copy(k).wait_recv()
            d = dh_s[rows(k)].astype(F32) + dh_r[rows(k)].astype(F32)
            route = jnp.sum(d * hid_v[rows(k)], axis=1, keepdims=True)
            route = jnp.broadcast_to(route, (cap, LANES)).astype(BF16)
            a = meta_r[rows(k)].astype(F32)[:, 0:1] * d
            dg[rows(k)] = (a * slope[rows(k)]).astype(BF16)
            du[rows(k)] = (a * act_v[rows(k)]).astype(BF16)
            if k:
                rt_s[rows(k)] = route
                rt_copy(k).start()
            else:
                rt_r[rows(0)] = route
        both = pl.ds(lo, 2 * cap)
        for j in range(nb):
            v = dot(dg[both], wg[cols(j)], 1, 1) + dot(du[both], wu[cols(j)], 1, 1)
            v = v.astype(BF16)
            dx[j, both] = v
            for k in pair:
                if k:
                    back_copy(k, j).start()

    far_step(0)
    end_next(2)
    w_in[1].wait()
    w_in[2].wait()
    input_grad((2, 3))
    end_next(3)
    inner_step(0)
    far_step(1)
    input_grad((1, 0))
    for j in range(2, nb):
        inner_step(j - 1)
        far_step(j)
    inner_step(nb - 1)

    for j in range(nb):
        v = dot(onehot_t[0, :, :cap], dx[j, rows(0)])
        for k in (1, 2, 3):
            back_copy(k, j).wait_recv()
            v = v + dot(onehot_t[k, :, :cap], back[j, rows(k)])
        tg_ref[:, cols(j)] = v.astype(BF16)
    v0 = jnp.zeros((tokens, LANES), F32)
    v1 = jnp.zeros((tokens, LANES), F32)
    for k in range(4):
        if k:
            rt_copy(k).wait_recv()
        r = dot(onehot_t[k, :, :cap], rt_r[rows(k)])
        v0 = v0 + jnp.where(first == peer[k], r, 0.0)
        v1 = v1 + jnp.where(second == peer[k], r, 0.0)
    pg_ref[...] = jnp.where(lane == 0, v0, v1)[:, :2].astype(BF16)

    own = z
    for j in range(nb):
        hold = dh.at[pl.ds(0, piece), pl.ds(0, bw)]
        hold[...] = product(own, j)

        @pl.when((z == 1) | (z == n_z - 2))
        def _():
            hold[...] += far_product(own, j)

        @pl.when(z > 1)
        def _():
            up_copy(own, j).wait_recv()
            hold[...] += up_r[own, j].astype(F32)

        @pl.when(z < n_z - 2)
        def _():
            lo_copy(own, j).wait_recv()
            hold[...] += lo_r[own, j].astype(F32)

        gd_ref[:, cols(j)] = hold[...].astype(BF16)

    for k in (1, 2, 3):
        meta_copy(k).wait_send()
        rt_copy(k).wait_send()
        for j in range(nb):
            disp_copy(k, j).wait_send()
            back_copy(k, j).wait_send()
    for k in range(4):
        dh_copy(k).wait_send()
    for d in range(n_z):
        for j in range(nb):
            @pl.when((z > 0) & (z < d))
            def _():
                up_copy(d, j).wait_send()

            @pl.when((z < n_z - 1) & (z > d))
            def _():
                lo_copy(d, j).wait_send()

    def ends_sent(step):
        end_hp_copy(step).wait_send()
        for j in range(nb - 2, nb):
            end_copy(j, step).wait_send()

    at_ends(ends_sent)


def fused_shards(n_z, grad_out, route_ids, route_probs, saved_pre, w_gate, w_up, w_down):
    tok, width = grad_out.shape
    slot_rows = saved_pre.shape[2]
    cap = slot_rows // 4
    hidden = saved_pre.shape[3] // 2
    nb = 4
    bw = width // nb
    piece = hidden // n_z
    names = jnp.concatenate([route_ids.astype(F32), route_probs.astype(F32)], axis=1)
    vmem = pl.BlockSpec(memory_space=pltpu.VMEM)
    hbm = pl.BlockSpec(memory_space=pl.ANY)
    dma = pltpu.SemaphoreType.DMA
    blocks = (nb, slot_rows, bw)
    hops = (n_z, nb, piece, bw)
    return pl.pallas_call(
        functools.partial(fused, n_z, cap, nb),
        out_shape=(
            jax.ShapeDtypeStruct((tok, width), BF16),
            jax.ShapeDtypeStruct(route_probs.shape, BF16),
            jax.ShapeDtypeStruct((piece, width), BF16),
        ),
        in_specs=[vmem, hbm, hbm, hbm, hbm, hbm],
        out_specs=(vmem, vmem, vmem),
        scratch_shapes=[
            pltpu.VMEM((tok, width), BF16),
            pltpu.VMEM((slot_rows, 2 * hidden), BF16),
            pltpu.VMEM((width, hidden), BF16),
            pltpu.VMEM((width, hidden), BF16),
            pltpu.VMEM((hidden, width), BF16),
            pltpu.VMEM((4, tok, LANES), BF16),
            pltpu.VMEM((slot_rows, LANES), BF16),
            pltpu.VMEM((slot_rows, LANES), BF16),
            pltpu.VMEM(blocks, BF16),
            pltpu.VMEM(blocks, BF16),
            pltpu.VMEM((slot_rows, hidden), F32),
            pltpu.VMEM((slot_rows, hidden), F32),
            pltpu.VMEM((slot_rows, hidden), F32),
            pltpu.VMEM((slot_rows, hidden), F32),
            pltpu.VMEM((hidden, slot_rows), BF16),
            pltpu.VMEM((slot_rows, hidden), F32),
            pltpu.VMEM((slot_rows, hidden), BF16),
            pltpu.VMEM((slot_rows, hidden), BF16),
            pltpu.VMEM((slot_rows, hidden), BF16),
            pltpu.VMEM((slot_rows, hidden), BF16),
            pltpu.VMEM(blocks, BF16),
            pltpu.VMEM(blocks, BF16),
            pltpu.VMEM((slot_rows, LANES), BF16),
            pltpu.VMEM((slot_rows, LANES), BF16),
            pltpu.VMEM(hops, BF16),
            pltpu.VMEM(hops, BF16),
            pltpu.VMEM(hops, BF16),
            pltpu.VMEM(hops, BF16),
            pltpu.VMEM(blocks, BF16),
            pltpu.VMEM((hidden, slot_rows), BF16),
            dma((nb,)), dma((4,)), dma((3,)),
            dma((4,)), dma((4,)), dma((4, nb)), dma((4, nb)), dma((4,)), dma((4,)),
            dma((4, nb)), dma((4, nb)), dma((4,)), dma((4,)),
            dma((n_z, nb)), dma((n_z, nb)), dma((n_z, nb)), dma((n_z, nb)), dma((nb + 1,)), dma((nb + 1,)),
        ],
        compiler_params=pltpu.CompilerParams(
            collective_id=0, has_side_effects=True, vmem_limit_bytes=56 * 1024 * 1024
        ),
    )(names, grad_out, saved_pre[0, 0], w_gate[0], w_up[0], w_down[0])


def takes_fused(shape, width, hidden, capacity):
    return (
        shape["expert"] == 4 and shape["tensor"] == 2 and shape["dp"] > 3 and capacity % 16 == 0 and capacity <= LANES
        and width % (4 * LANES) == 0 and hidden % LANES == 0 and (hidden // shape["dp"]) % 16 == 0
    )


def slot_index(id_block, n_experts, capacity):
    flat = id_block.reshape(-1)
    onehot = (flat[:, None] == jnp.arange(n_experts, dtype=jnp.int32)[None, :]).astype(jnp.int32)
    before = jnp.cumsum(onehot, axis=0) - onehot
    position = jnp.sum(before * onehot, axis=1)
    return flat * capacity + position


def backward_rows(dh_rows, gate, upper, sig, act, hid, p32):
    route = jnp.sum(dh_rows * hid, axis=1).astype(jnp.bfloat16)
    scaled = p32 * dh_rows
    dgate = (scaled * upper * sig * (1.0 + gate * (1.0 - sig))).astype(jnp.bfloat16)
    dup = (scaled * act).astype(jnp.bfloat16)
    return (dgate, dup, route)


def shards(grad_out, route_ids, route_probs, saved_pre, w_gate, w_up, w_down):
    n_exp = lax.axis_size("expert")
    slot_rows = saved_pre.shape[2]
    capacity = slot_rows // n_exp
    tok = grad_out.shape[0]
    topk = route_ids.shape[1]
    width = grad_out.shape[1]
    hidden = saved_pre.shape[3] // 2
    slots = slot_index(route_ids, n_exp, capacity)
    source = (
        jnp.zeros((n_exp * capacity,), jnp.int32)
        .at[slots]
        .set(jnp.arange(tok * topk, dtype=jnp.int32) + 1)
    )
    valid = source > 0
    flat_src = jnp.maximum(source - 1, 0)
    send_rows = jnp.where(valid[:, None], grad_out[flat_src // topk], jnp.zeros((), jnp.bfloat16))
    send_prob = jnp.where(valid, route_probs.reshape(-1)[flat_src], jnp.zeros((), jnp.bfloat16))
    got_rows, got_prob = (
        lax.all_to_all(
            send_rows.reshape(n_exp, capacity, width),
            "expert",
            split_axis=0,
            concat_axis=0,
            tiled=True,
        ),
        lax.all_to_all(
            send_prob.reshape(n_exp, capacity), "expert", split_axis=0, concat_axis=0, tiled=True
        ),
    )
    dyr = got_rows.reshape(slot_rows, width)
    p32 = got_prob.reshape(slot_rows, 1).astype(jnp.float32)
    pre = saved_pre[0, 0]
    gate = pre[:, :hidden].astype(jnp.float32)
    upper = pre[:, hidden:].astype(jnp.float32)
    sig = jax.nn.sigmoid(gate)
    act = gate * sig
    hid = act * upper
    hpro = (p32 * hid).astype(jnp.bfloat16)
    down_term = lax.dot_general(
        hpro, dyr, (((0,), (0,)), ((), ())), preferred_element_type=jnp.float32
    )
    dh_part = lax.dot_general(
        dyr, w_down[0], (((1,), (1,)), ((), ())), preferred_element_type=jnp.float32
    )
    dh_rows = lax.psum(dh_part.astype(jnp.bfloat16), "tensor").astype(jnp.float32)
    dgate, dup, route = backward_rows(dh_rows, gate, upper, sig, act, hid, p32)
    dx = lax.dot_general(
        dgate, w_gate[0], (((1,), (1,)), ((), ())), preferred_element_type=jnp.float32
    )
    dx = dx + lax.dot_general(
        dup, w_up[0], (((1,), (1,)), ((), ())), preferred_element_type=jnp.float32
    )
    dx = dx.astype(jnp.bfloat16)
    back_rows, back_route = (
        lax.all_to_all(
            dx.reshape(n_exp, capacity, width), "expert", split_axis=0, concat_axis=0, tiled=True
        ),
        lax.all_to_all(
            route.reshape(n_exp, capacity), "expert", split_axis=0, concat_axis=0, tiled=True
        ),
    )
    picked = back_rows.reshape(n_exp * capacity, width)[slots].reshape(tok, topk, width)
    token_grad = jnp.sum(picked.astype(jnp.float32), axis=1).astype(jnp.bfloat16)
    prob_grad = back_route.reshape(n_exp * capacity)[slots].reshape(tok, topk)
    grad_down = lax.psum_scatter(
        down_term[None].astype(jnp.bfloat16), "dp", scatter_dimension=1, tiled=True
    )
    return (token_grad, prob_grad, grad_down)


def solution(mesh):
    shape = dict(mesh.shape)

    def local(*args):
        saved_pre, w_down = args[3], args[6]
        capacity = saved_pre.shape[2] // shape["expert"]
        tok = args[0].shape[0]
        if tok == LANES and takes_fused(shape, w_down.shape[2], w_down.shape[1], capacity):
            return tuple(
                v[None] if i == 2 else v for i, v in enumerate(fused_shards(shape["dp"], *args))
            )
        return shards(*args)

    return jax.shard_map(
        local,
        mesh=mesh,
        in_specs=(
            P(("dp", "expert"), "tensor"),
            P(("dp", "expert"), None),
            P(("dp", "expert"), None),
            P("dp", "expert", None, None),
            P("expert", "tensor", None),
            P("expert", "tensor", None),
            P("expert", None, "tensor"),
        ),
        out_specs=(
            P(("dp", "expert"), "tensor"),
            P(("dp", "expert"), None),
            P("expert", "dp", "tensor"),
        ),
        check_vma=False,
    )
```

```python
import functools

import jax
import jax.numpy as jnp
from jax import lax
from jax.experimental import pallas as pl
from jax.experimental.pallas import tpu as pltpu
from jax.sharding import PartitionSpec as P

MESH = pl.DeviceIdType.MESH
BF16, F32 = jnp.bfloat16, jnp.float32
LANES = 128
BLOCKS = 8


def dot(a, b, ca=1, cb=0):
    return lax.dot_general(a, b, (((ca,), (cb,)), ((), ())), preferred_element_type=F32)


def fused(
    n_z, cap, nb,
    ids_ref, prob_ref, tok_hbm, pre_hbm, wg_hbm, wu_hbm, wd_hbm,
    tg_ref, pg_ref, gd_ref,
    tok, pre, wg, wu, wd,
    onehot_t, meta_s, meta_r, rows_s, disp,
    slope, act_v, hid_v, hp, hp_t,
    dh, dh_s, dh_r, dg, du, dx, back, rt_s, rt_r,
    up_s, up_r, lo_s, lo_r, far_disp, far_hp,
    tok_sem, pre_sem, w_sem,
    meta_ss, meta_rs, disp_ss, disp_rs, dh_ss, dh_rs, back_ss, back_rs, rt_ss, rt_rs,
    up_ss, up_rs, lo_ss, lo_rs, end_ss, end_rs,
):
    z, me, x = lax.axis_index("dp"), lax.axis_index("expert"), lax.axis_index("tensor")
    peer = [me, me + 1 - 2 * (me % 2), (me + 2) % 4, 3 - me]
    far = (2, 3, 1)
    tokens, width = tok.shape[0], tok.shape[1]
    bw = width // nb
    hidden = wd.shape[0]
    piece = hidden // n_z
    q = nb // 4

    def rows(k):
        return pl.ds(k * cap, cap)

    def cols(j):
        return pl.ds(j * bw, bw)

    def to_peer(src, dst, ss, rs, k):
        return pltpu.make_async_remote_copy(src, dst, ss, rs, device_id={"expert": peer[k]}, device_id_type=MESH)

    def meta_copy(k):
        return to_peer(meta_s.at[rows(k)], meta_r.at[rows(k)], meta_ss.at[k], meta_rs.at[k], k)

    def disp_copy(k, j):
        return to_peer(rows_s.at[j, rows(k)], disp.at[j, rows(k)], disp_ss.at[k, j], disp_rs.at[k, j], k)

    def back_copy(k, j):
        return to_peer(dx.at[j, rows(k)], back.at[j, rows(k)], back_ss.at[k, j], back_rs.at[k, j], k)

    def rt_copy(k):
        return to_peer(rt_s.at[rows(k)], rt_r.at[rows(k)], rt_ss.at[k], rt_rs.at[k], k)

    def dh_copy(k):
        return pltpu.make_async_remote_copy(
            dh_s.at[rows(k)], dh_r.at[rows(k)], dh_ss.at[k], dh_rs.at[k],
            device_id={"tensor": 1 - x}, device_id_type=MESH)

    def up_copy(d, j):
        return pltpu.make_async_remote_copy(
            up_s.at[d, j], up_r.at[d, j], up_ss.at[d, j], up_rs.at[d, j],
            device_id={"dp": z + 1}, device_id_type=MESH)

    def lo_copy(d, j):
        return pltpu.make_async_remote_copy(
            lo_s.at[d, j], lo_r.at[d, j], lo_ss.at[d, j], lo_rs.at[d, j],
            device_id={"dp": z - 1}, device_id_type=MESH)

    def end_copy(j, step):
        return pltpu.make_async_remote_copy(
            disp.at[j], far_disp.at[j], end_ss.at[j], end_rs.at[j],
            device_id={"dp": z + step}, device_id_type=MESH)

    def end_hp_copy(step):
        part = pl.ds(piece if step > 0 else 0, hidden - piece)
        return pltpu.make_async_remote_copy(
            hp_t.at[part], far_hp.at[part], end_ss.at[nb], end_rs.at[nb],
            device_id={"dp": z + step}, device_id_type=MESH)

    def at_ends(act):
        @pl.when(z == 0)
        def _():
            act(1)

        @pl.when(z == n_z - 1)
        def _():
            act(-1)

    tok_in = [pltpu.make_async_copy(tok_hbm.at[:, cols(j)], tok.at[:, cols(j)], tok_sem.at[j]) for j in range(nb)]
    pre_in = [
        pltpu.make_async_copy(pre_hbm.at[pl.ds(pl.multiple_of(peer[k] * cap, 16), cap)], pre.at[rows(k)], pre_sem.at[k])
        for k in range(4)
    ]
    w_in = [
        pltpu.make_async_copy(wd_hbm, wd, w_sem.at[0]),
        pltpu.make_async_copy(wg_hbm, wg, w_sem.at[1]),
        pltpu.make_async_copy(wu_hbm, wu, w_sem.at[2]),
    ]
    for c in tok_in + pre_in + w_in:
        c.start()

    barrier = pltpu.get_barrier_semaphore()
    for k in (1, 2, 3):
        pl.semaphore_signal(barrier, inc=1, device_id={"expert": peer[k]}, device_id_type=MESH)
    pl.semaphore_signal(barrier, inc=1, device_id={"tensor": 1 - x}, device_id_type=MESH)

    @pl.when(z > 0)
    def _():
        pl.semaphore_signal(barrier, inc=1, device_id={"dp": z - 1}, device_id_type=MESH)

    @pl.when(z < n_z - 1)
    def _():
        pl.semaphore_signal(barrier, inc=1, device_id={"dp": z + 1}, device_id_type=MESH)

    lane = lax.broadcasted_iota(jnp.int32, (tokens, LANES), 1)
    row_i = lax.broadcasted_iota(jnp.int32, (tokens, tokens), 0)
    col_i = lax.broadcasted_iota(jnp.int32, (tokens, tokens), 1)
    lower = (col_i < row_i).astype(F32).astype(BF16)

    def column(ref, i):
        return jnp.broadcast_to(ref[i:i + 1, :].astype(F32), (tokens, tokens)).T

    first, second = column(ids_ref, 0).astype(jnp.int32), column(ids_ref, 1).astype(jnp.int32)
    prob0, prob1 = column(prob_ref, 0), column(prob_ref, 1)
    pick = []
    for k in range(4):
        m = ((first == peer[k]) | (second == peer[k])).astype(F32)
        mb = m
        pos = dot(lower, mb.astype(BF16))
        sel = jnp.where(pos == lane.astype(F32), mb, 0.0)
        onehot_t[k] = sel.astype(BF16)
        s = sel.T[:cap].astype(BF16)
        pick.append(s)
        pk = jnp.where(first == peer[k], prob0, jnp.where(second == peer[k], prob1, 0.0))
        meta = dot(s, pk.astype(BF16)).astype(BF16)
        if k == 0:
            meta_r[rows(0)] = meta
        else:
            meta_s[rows(k)] = meta

    @pl.when((z > 0) & (z < n_z - 1))
    def _():
        pl.semaphore_wait(barrier, 6)

    @pl.when((z == 0) | (z == n_z - 1))
    def _():
        pl.semaphore_wait(barrier, 5)

    for k in far:
        meta_copy(k).start()
    for j in range(nb):
        tok_in[j].wait()
        block = tok[:, cols(j)]
        for k in far:
            rows_s[j, rows(k)] = dot(pick[k], block).astype(BF16)
            disp_copy(k, j).start()
        disp[j, rows(0)] = dot(pick[0], block).astype(BF16)

    for k in range(4):
        pre_in[k].wait()
        if k:
            meta_copy(k).wait_recv()
        p = meta_r[rows(k)].astype(F32)[:, 0:1]
        g = pre[rows(k), :hidden].astype(F32)
        u = pre[rows(k), hidden:].astype(F32)
        sg = jax.nn.sigmoid(g)
        act = g * sg
        hid = act * u
        act_v[rows(k)] = act
        hid_v[rows(k)] = hid
        slope[rows(k)] = u * sg * (1.0 + g * (1.0 - sg))
        hp[rows(k)] = p * hid
    for h in range(0, hidden, LANES):
        hp_t[pl.ds(h, LANES)] = hp[:, pl.ds(h, LANES)].T.astype(BF16)

    def product(d, j):
        return dot(hp_t[pl.ds(pl.multiple_of(d * piece, 16), piece)], disp[j])

    def far_product(d, j):
        return dot(far_hp[pl.ds(pl.multiple_of(d * piece, 16), piece)], far_disp[j])

    def send_up(d, j, inner):
        v = product(d, j)
        if inner:
            up_copy(d, j).wait_recv()
            v = v + up_r[d, j].astype(F32)
        else:
            v = v + far_product(d, j)
        up_s[d, j] = v.astype(BF16)
        up_copy(d, j).start()

    def send_lo(d, j, inner):
        v = product(d, j)
        if inner:
            lo_copy(d, j).wait_recv()
            v = v + lo_r[d, j].astype(F32)
        else:
            v = v + far_product(d, j)
        lo_s[d, j] = v.astype(BF16)
        lo_copy(d, j).start()

    at_ends(lambda step: end_hp_copy(step).start())
    w_in[0].wait()
    for j in range(nb):
        for k in far:
            disp_copy(k, j).wait_recv()

        if j < 2 * q:
            at_ends(lambda step: end_copy(j, step).start())
        part = dot(disp[j], wd[:, cols(j)], 1, 1)
        if j == 0:
            dh[...] = part
        elif j < nb - 1:
            dh[...] += part
        else:
            part = (dh[...] + part).astype(BF16)
            dh_s[...] = part
    for k in (2, 3, 1, 0):
        dh_copy(k).start()

    def end_next(j):
        def go(step):
            end_copy(j - 2 * q, step).wait_send()
            end_copy(j, step).start()

        at_ends(go)

    def far_step(j):
        @pl.when(z == 1)
        def _():
            if j == 0:
                end_hp_copy(1).wait_recv()
            end_copy(j, 1).wait_recv()
            for d in range(n_z - 1, 1, -1):
                send_up(d, j, False)

        @pl.when(z == n_z - 2)
        def _():
            if j == 0:
                end_hp_copy(-1).wait_recv()
            end_copy(j, -1).wait_recv()
            for d in range(n_z - 2):
                send_lo(d, j, False)

    def inner_step(j):
        for t in range(n_z - 3):
            @pl.when((z > 1) & (z < n_z - 1 - t))
            def _():
                send_up(n_z - 1 - t, j, True)

            @pl.when((z < n_z - 2) & (z > t))
            def _():
                send_lo(t, j, True)

    def input_grad(pair):
        lo = min(pair) * cap
        for k in pair:
            dh_copy(k).wait_recv()
            d = dh_s[rows(k)].astype(F32) + dh_r[rows(k)].astype(F32)
            route = jnp.sum(d * hid_v[rows(k)], axis=1, keepdims=True)
            route = jnp.broadcast_to(route, (cap, LANES)).astype(BF16)
            a = meta_r[rows(k)].astype(F32)[:, 0:1] * d
            dg[rows(k)] = (a * slope[rows(k)]).astype(BF16)
            du[rows(k)] = (a * act_v[rows(k)]).astype(BF16)
            if k:
                rt_s[rows(k)] = route
                rt_copy(k).start()
            else:
                rt_r[rows(0)] = route
        both = pl.ds(lo, 2 * cap)
        for j in range(nb):
            v = dot(dg[both], wg[cols(j)], 1, 1) + dot(du[both], wu[cols(j)], 1, 1)
            v = v.astype(BF16)
            dx[j, both] = v
            for k in pair:
                if k:
                    back_copy(k, j).start()

    for j in range(q):
        far_step(j)
        end_next(2 * q + j)
    w_in[1].wait()
    w_in[2].wait()
    input_grad((2, 3))
    for j in range(q):
        end_next(3 * q + j)
        inner_step(j)
        far_step(q + j)
    input_grad((1, 0))
    for j in range(2 * q, nb):
        inner_step(j - q)
        far_step(j)
    for j in range(nb - q, nb):
        inner_step(j)

    for j in range(nb):
        v = dot(onehot_t[0, :, :cap], dx[j, rows(0)])
        for k in (1, 2, 3):
            back_copy(k, j).wait_recv()
            v = v + dot(onehot_t[k, :, :cap], back[j, rows(k)])
        tg_ref[:, cols(j)] = v.astype(BF16)
    v0 = jnp.zeros((tokens, LANES), F32)
    v1 = jnp.zeros((tokens, LANES), F32)
    for k in range(4):
        if k:
            rt_copy(k).wait_recv()
        r = dot(onehot_t[k, :, :cap], rt_r[rows(k)])
        v0 = v0 + jnp.where(first == peer[k], r, 0.0)
        v1 = v1 + jnp.where(second == peer[k], r, 0.0)
    pg_ref[...] = jnp.where(row_i == 0, v0.T, v1.T)[:2].astype(BF16)

    own = z
    for j in range(nb):
        hold = dh.at[pl.ds(0, piece), pl.ds(0, bw)]
        hold[...] = product(own, j)

        @pl.when((z == 1) | (z == n_z - 2))
        def _():
            hold[...] += far_product(own, j)

        @pl.when(z > 1)
        def _():
            up_copy(own, j).wait_recv()
            hold[...] += up_r[own, j].astype(F32)

        @pl.when(z < n_z - 2)
        def _():
            lo_copy(own, j).wait_recv()
            hold[...] += lo_r[own, j].astype(F32)

        gd_ref[:, cols(j)] = hold[...].astype(BF16)

    for k in (1, 2, 3):
        meta_copy(k).wait_send()
        rt_copy(k).wait_send()
        for j in range(nb):
            disp_copy(k, j).wait_send()
            back_copy(k, j).wait_send()
    for k in range(4):
        dh_copy(k).wait_send()
    for d in range(n_z):
        for j in range(nb):
            @pl.when((z > 0) & (z < d))
            def _():
                up_copy(d, j).wait_send()

            @pl.when((z < n_z - 1) & (z > d))
            def _():
                lo_copy(d, j).wait_send()

    def ends_sent(step):
        end_hp_copy(step).wait_send()
        for j in range(nb - 2 * q, nb):
            end_copy(j, step).wait_send()

    at_ends(ends_sent)


def fused_shards(n_z, grad_out, route_ids, route_probs, saved_pre, w_gate, w_up, w_down):
    tok, width = grad_out.shape
    slot_rows = saved_pre.shape[2]
    cap = slot_rows // 4
    hidden = saved_pre.shape[3] // 2
    nb = BLOCKS
    bw = width // nb
    piece = hidden // n_z
    vmem = pl.BlockSpec(memory_space=pltpu.VMEM)
    hbm = pl.BlockSpec(memory_space=pl.ANY)
    dma = pltpu.SemaphoreType.DMA
    blocks = (nb, slot_rows, bw)
    hops = (n_z, nb, piece, bw)
    return pl.pallas_call(
        functools.partial(fused, n_z, cap, nb),
        out_shape=(
            jax.ShapeDtypeStruct((tok, width), BF16),
            jax.ShapeDtypeStruct(route_probs.shape[::-1], BF16),
            jax.ShapeDtypeStruct((piece, width), BF16),
        ),
        in_specs=[vmem, vmem, hbm, hbm, hbm, hbm, hbm],
        out_specs=(vmem, vmem, vmem),
        scratch_shapes=[
            pltpu.VMEM((tok, width), BF16),
            pltpu.VMEM((slot_rows, 2 * hidden), BF16),
            pltpu.VMEM((width, hidden), BF16),
            pltpu.VMEM((width, hidden), BF16),
            pltpu.VMEM((hidden, width), BF16),
            pltpu.VMEM((4, tok, LANES), BF16),
            pltpu.VMEM((slot_rows, LANES), BF16),
            pltpu.VMEM((slot_rows, LANES), BF16),
            pltpu.VMEM(blocks, BF16),
            pltpu.VMEM(blocks, BF16),
            pltpu.VMEM((slot_rows, hidden), F32),
            pltpu.VMEM((slot_rows, hidden), F32),
            pltpu.VMEM((slot_rows, hidden), F32),
            pltpu.VMEM((slot_rows, hidden), F32),
            pltpu.VMEM((hidden, slot_rows), BF16),
            pltpu.VMEM((slot_rows, hidden), F32),
            pltpu.VMEM((slot_rows, hidden), BF16),
            pltpu.VMEM((slot_rows, hidden), BF16),
            pltpu.VMEM((slot_rows, hidden), BF16),
            pltpu.VMEM((slot_rows, hidden), BF16),
            pltpu.VMEM(blocks, BF16),
            pltpu.VMEM(blocks, BF16),
            pltpu.VMEM((slot_rows, LANES), BF16),
            pltpu.VMEM((slot_rows, LANES), BF16),
            pltpu.VMEM(hops, BF16),
            pltpu.VMEM(hops, BF16),
            pltpu.VMEM(hops, BF16),
            pltpu.VMEM(hops, BF16),
            pltpu.VMEM(blocks, BF16),
            pltpu.VMEM((hidden, slot_rows), BF16),
            dma((nb,)), dma((4,)), dma((3,)),
            dma((4,)), dma((4,)), dma((4, nb)), dma((4, nb)), dma((4,)), dma((4,)),
            dma((4, nb)), dma((4, nb)), dma((4,)), dma((4,)),
            dma((n_z, nb)), dma((n_z, nb)), dma((n_z, nb)), dma((n_z, nb)), dma((nb + 1,)), dma((nb + 1,)),
        ],
        compiler_params=pltpu.CompilerParams(
            collective_id=0, has_side_effects=True, vmem_limit_bytes=56 * 1024 * 1024
        ),
    )(route_ids.T, route_probs.T, grad_out, saved_pre[0, 0], w_gate[0], w_up[0], w_down[0])


def takes_fused(shape, width, hidden, capacity):
    return (
        shape["expert"] == 4 and shape["tensor"] == 2 and shape["dp"] > 3 and capacity % 16 == 0 and capacity <= LANES
        and width % (BLOCKS * LANES) == 0 and hidden % LANES == 0 and (hidden // shape["dp"]) % 16 == 0
    )


def slot_index(id_block, n_experts, capacity):
    flat = id_block.reshape(-1)
    onehot = (flat[:, None] == jnp.arange(n_experts, dtype=jnp.int32)[None, :]).astype(jnp.int32)
    before = jnp.cumsum(onehot, axis=0) - onehot
    position = jnp.sum(before * onehot, axis=1)
    return flat * capacity + position


def backward_rows(dh_rows, gate, upper, sig, act, hid, p32):
    route = jnp.sum(dh_rows * hid, axis=1).astype(jnp.bfloat16)
    scaled = p32 * dh_rows
    dgate = (scaled * upper * sig * (1.0 + gate * (1.0 - sig))).astype(jnp.bfloat16)
    dup = (scaled * act).astype(jnp.bfloat16)
    return (dgate, dup, route)


def shards(grad_out, route_ids, route_probs, saved_pre, w_gate, w_up, w_down):
    n_exp = lax.axis_size("expert")
    slot_rows = saved_pre.shape[2]
    capacity = slot_rows // n_exp
    tok = grad_out.shape[0]
    topk = route_ids.shape[1]
    width = grad_out.shape[1]
    hidden = saved_pre.shape[3] // 2
    slots = slot_index(route_ids, n_exp, capacity)
    source = (
        jnp.zeros((n_exp * capacity,), jnp.int32)
        .at[slots]
        .set(jnp.arange(tok * topk, dtype=jnp.int32) + 1)
    )
    valid = source > 0
    flat_src = jnp.maximum(source - 1, 0)
    send_rows = jnp.where(valid[:, None], grad_out[flat_src // topk], jnp.zeros((), jnp.bfloat16))
    send_prob = jnp.where(valid, route_probs.reshape(-1)[flat_src], jnp.zeros((), jnp.bfloat16))
    got_rows, got_prob = (
        lax.all_to_all(
            send_rows.reshape(n_exp, capacity, width),
            "expert",
            split_axis=0,
            concat_axis=0,
            tiled=True,
        ),
        lax.all_to_all(
            send_prob.reshape(n_exp, capacity), "expert", split_axis=0, concat_axis=0, tiled=True
        ),
    )
    dyr = got_rows.reshape(slot_rows, width)
    p32 = got_prob.reshape(slot_rows, 1).astype(jnp.float32)
    pre = saved_pre[0, 0]
    gate = pre[:, :hidden].astype(jnp.float32)
    upper = pre[:, hidden:].astype(jnp.float32)
    sig = jax.nn.sigmoid(gate)
    act = gate * sig
    hid = act * upper
    hpro = (p32 * hid).astype(jnp.bfloat16)
    down_term = lax.dot_general(
        hpro, dyr, (((0,), (0,)), ((), ())), preferred_element_type=jnp.float32
    )
    dh_part = lax.dot_general(
        dyr, w_down[0], (((1,), (1,)), ((), ())), preferred_element_type=jnp.float32
    )
    dh_rows = lax.psum(dh_part.astype(jnp.bfloat16), "tensor").astype(jnp.float32)
    dgate, dup, route = backward_rows(dh_rows, gate, upper, sig, act, hid, p32)
    dx = lax.dot_general(
        dgate, w_gate[0], (((1,), (1,)), ((), ())), preferred_element_type=jnp.float32
    )
    dx = dx + lax.dot_general(
        dup, w_up[0], (((1,), (1,)), ((), ())), preferred_element_type=jnp.float32
    )
    dx = dx.astype(jnp.bfloat16)
    back_rows, back_route = (
        lax.all_to_all(
            dx.reshape(n_exp, capacity, width), "expert", split_axis=0, concat_axis=0, tiled=True
        ),
        lax.all_to_all(
            route.reshape(n_exp, capacity), "expert", split_axis=0, concat_axis=0, tiled=True
        ),
    )
    picked = back_rows.reshape(n_exp * capacity, width)[slots].reshape(tok, topk, width)
    token_grad = jnp.sum(picked.astype(jnp.float32), axis=1).astype(jnp.bfloat16)
    prob_grad = back_route.reshape(n_exp * capacity)[slots].reshape(tok, topk)
    grad_down = lax.psum_scatter(
        down_term[None].astype(jnp.bfloat16), "dp", scatter_dimension=1, tiled=True
    )
    return (token_grad, prob_grad, grad_down)


def solution(mesh):
    shape = dict(mesh.shape)

    def local(*args):
        saved_pre, w_down = args[3], args[6]
        capacity = saved_pre.shape[2] // shape["expert"]
        tok = args[0].shape[0]
        if tok == LANES and takes_fused(shape, w_down.shape[2], w_down.shape[1], capacity):
            return tuple(
                v[None] if i == 2 else v.T if i == 1 else v for i, v in enumerate(fused_shards(shape["dp"], *args))
            )
        return shards(*args)

    return jax.shard_map(
        local,
        mesh=mesh,
        in_specs=(
            P(("dp", "expert"), "tensor"),
            P(("dp", "expert"), None),
            P(("dp", "expert"), None),
            P("dp", "expert", None, None),
            P("expert", "tensor", None),
            P("expert", "tensor", None),
            P("expert", None, "tensor"),
        ),
        out_specs=(
            P(("dp", "expert"), "tensor"),
            P(("dp", "expert"), None),
            P("expert", "dp", "tensor"),
        ),
        check_vma=False,
    )
```

```python
import functools

import jax
import jax.numpy as jnp
from jax import lax
from jax.experimental import pallas as pl
from jax.experimental.pallas import tpu as pltpu
from jax.sharding import PartitionSpec as P

MESH = pl.DeviceIdType.MESH
BF16, F32 = jnp.bfloat16, jnp.float32
LANES = 128
BLOCKS = 4


def dot(a, b, ca=1, cb=0):
    return lax.dot_general(a, b, (((ca,), (cb,)), ((), ())), preferred_element_type=F32)


def fused(
    n_z, cap, nb,
    ids_ref, prob_ref, tok_hbm, pre_hbm, wg_hbm, wu_hbm, wd_hbm,
    tg_ref, pg_ref, gd_ref,
    tok, pre, wg, wu, wd,
    onehot_t, meta_s, meta_r, rows_s, disp,
    slope, act_v, hid_v, hp, hp_t,
    dh, dh_s, dh_r, dg, du, dx, back, rt_s, rt_r,
    up_s, up_r, lo_s, lo_r, far_disp, far_hp,
    tok_sem, pre_sem, w_sem,
    meta_ss, meta_rs, disp_ss, disp_rs, dh_ss, dh_rs, back_ss, back_rs, rt_ss, rt_rs,
    up_ss, up_rs, lo_ss, lo_rs, end_ss, end_rs,
):
    z, me, x = lax.axis_index("dp"), lax.axis_index("expert"), lax.axis_index("tensor")
    peer = [me, me + 1 - 2 * (me % 2), (me + 2) % 4, 3 - me]
    far = (2, 3, 1)
    tokens, width = tok.shape[0], tok.shape[1]
    bw = width // nb
    hidden = wd.shape[0]
    piece = hidden // n_z
    q = nb // 4

    def rows(k):
        return pl.ds(k * cap, cap)

    def cols(j):
        return pl.ds(j * bw, bw)

    def to_peer(src, dst, ss, rs, k):
        return pltpu.make_async_remote_copy(src, dst, ss, rs, device_id={"expert": peer[k]}, device_id_type=MESH)

    def meta_copy(k):
        return to_peer(meta_s.at[rows(k)], meta_r.at[rows(k)], meta_ss.at[k], meta_rs.at[k], k)

    def disp_copy(k, j):
        return to_peer(rows_s.at[j, rows(k)], disp.at[j, rows(k)], disp_ss.at[k, j], disp_rs.at[k, j], k)

    def back_copy(k, j):
        return to_peer(dx.at[j, rows(k)], back.at[j, rows(k)], back_ss.at[k, j], back_rs.at[k, j], k)

    def rt_copy(k):
        return to_peer(rt_s.at[rows(k)], rt_r.at[rows(k)], rt_ss.at[k], rt_rs.at[k], k)

    def dh_copy(k):
        return pltpu.make_async_remote_copy(
            dh_s.at[rows(k)], dh_r.at[rows(k)], dh_ss.at[k], dh_rs.at[k],
            device_id={"tensor": 1 - x}, device_id_type=MESH)

    def up_copy(d, j):
        return pltpu.make_async_remote_copy(
            up_s.at[d, j], up_r.at[d, j], up_ss.at[d, j], up_rs.at[d, j],
            device_id={"dp": z + 1}, device_id_type=MESH)

    def lo_copy(d, j):
        return pltpu.make_async_remote_copy(
            lo_s.at[d, j], lo_r.at[d, j], lo_ss.at[d, j], lo_rs.at[d, j],
            device_id={"dp": z - 1}, device_id_type=MESH)

    def end_copy(j, step):
        return pltpu.make_async_remote_copy(
            disp.at[j], far_disp.at[j], end_ss.at[j], end_rs.at[j],
            device_id={"dp": z + step}, device_id_type=MESH)

    def end_hp_copy(step):
        part = pl.ds(piece if step > 0 else 0, hidden - piece)
        return pltpu.make_async_remote_copy(
            hp_t.at[part], far_hp.at[part], end_ss.at[nb], end_rs.at[nb],
            device_id={"dp": z + step}, device_id_type=MESH)

    def at_ends(act):
        @pl.when(z == 0)
        def _():
            act(1)

        @pl.when(z == n_z - 1)
        def _():
            act(-1)

    tok_in = [pltpu.make_async_copy(tok_hbm.at[:, cols(j)], tok.at[:, cols(j)], tok_sem.at[j]) for j in range(nb)]
    pre_in = [
        pltpu.make_async_copy(pre_hbm.at[pl.ds(pl.multiple_of(peer[k] * cap, 16), cap)], pre.at[rows(k)], pre_sem.at[k])
        for k in range(4)
    ]
    w_in = [
        pltpu.make_async_copy(wd_hbm, wd, w_sem.at[0]),
        pltpu.make_async_copy(wg_hbm, wg, w_sem.at[1]),
        pltpu.make_async_copy(wu_hbm, wu, w_sem.at[2]),
    ]
    for c in tok_in + pre_in + w_in:
        c.start()

    barrier = pltpu.get_barrier_semaphore()
    for k in (1, 2, 3):
        pl.semaphore_signal(barrier, inc=1, device_id={"expert": peer[k]}, device_id_type=MESH)
    pl.semaphore_signal(barrier, inc=1, device_id={"tensor": 1 - x}, device_id_type=MESH)

    @pl.when(z > 0)
    def _():
        pl.semaphore_signal(barrier, inc=1, device_id={"dp": z - 1}, device_id_type=MESH)

    @pl.when(z < n_z - 1)
    def _():
        pl.semaphore_signal(barrier, inc=1, device_id={"dp": z + 1}, device_id_type=MESH)

    lane = lax.broadcasted_iota(jnp.int32, (tokens, LANES), 1)
    row_i = lax.broadcasted_iota(jnp.int32, (tokens, tokens), 0)
    col_i = lax.broadcasted_iota(jnp.int32, (tokens, tokens), 1)
    lower = (col_i < row_i).astype(F32).astype(BF16)

    def column(ref, i):
        return jnp.broadcast_to(ref[i:i + 1, :].astype(F32), (tokens, tokens)).T

    first, second = column(ids_ref, 0).astype(jnp.int32), column(ids_ref, 1).astype(jnp.int32)
    prob0, prob1 = column(prob_ref, 0), column(prob_ref, 1)
    pick = []
    for k in range(4):
        m = ((first == peer[k]) | (second == peer[k])).astype(F32)
        mb = m
        pos = dot(lower, mb.astype(BF16))
        sel = jnp.where(pos == lane.astype(F32), mb, 0.0)
        onehot_t[k] = sel.astype(BF16)
        s = sel.T[:cap].astype(BF16)
        pick.append(s)
        pk = jnp.where(first == peer[k], prob0, jnp.where(second == peer[k], prob1, 0.0))
        meta = dot(s, pk.astype(BF16)).astype(BF16)
        if k == 0:
            meta_r[rows(0)] = meta
        else:
            meta_s[rows(k)] = meta

    @pl.when((z > 0) & (z < n_z - 1))
    def _():
        pl.semaphore_wait(barrier, 6)

    @pl.when((z == 0) | (z == n_z - 1))
    def _():
        pl.semaphore_wait(barrier, 5)

    for k in far:
        meta_copy(k).start()
    for j in range(nb):
        tok_in[j].wait()
        block = tok[:, cols(j)]
        for k in far:
            rows_s[j, rows(k)] = dot(pick[k], block).astype(BF16)
            disp_copy(k, j).start()
        disp[j, rows(0)] = dot(pick[0], block).astype(BF16)

    for k in range(4):
        pre_in[k].wait()
        if k:
            meta_copy(k).wait_recv()
        p = meta_r[rows(k)].astype(F32)[:, 0:1]
        g = pre[rows(k), :hidden].astype(F32)
        u = pre[rows(k), hidden:].astype(F32)
        sg = jax.nn.sigmoid(g)
        act = g * sg
        hid = act * u
        act_v[rows(k)] = act
        hid_v[rows(k)] = hid
        slope[rows(k)] = u * sg * (1.0 + g * (1.0 - sg))
        hp[rows(k)] = p * hid
    for h in range(0, hidden, LANES):
        hp_t[pl.ds(h, LANES)] = hp[:, pl.ds(h, LANES)].T.astype(BF16)

    def product(d, j):
        return dot(hp_t[pl.ds(pl.multiple_of(d * piece, 16), piece)], disp[j])

    def far_product(d, j):
        return dot(far_hp[pl.ds(pl.multiple_of(d * piece, 16), piece)], far_disp[j])

    def send_up(d, j, inner):
        v = product(d, j)
        if inner:
            up_copy(d, j).wait_recv()
            v = v + up_r[d, j].astype(F32)
        else:
            v = v + far_product(d, j)
        up_s[d, j] = v.astype(BF16)
        up_copy(d, j).start()

    def send_lo(d, j, inner):
        v = product(d, j)
        if inner:
            lo_copy(d, j).wait_recv()
            v = v + lo_r[d, j].astype(F32)
        else:
            v = v + far_product(d, j)
        lo_s[d, j] = v.astype(BF16)
        lo_copy(d, j).start()

    at_ends(lambda step: end_hp_copy(step).start())
    w_in[0].wait()
    for j in range(nb):
        for k in far:
            disp_copy(k, j).wait_recv()

        if j < 2 * q:
            at_ends(lambda step: end_copy(j, step).start())
        part = dot(disp[j], wd[:, cols(j)], 1, 1)
        if j == 0:
            dh[...] = part
        elif j < nb - 1:
            dh[...] += part
        else:
            part = (dh[...] + part).astype(BF16)
            dh_s[...] = part
    for k in (2, 3, 1, 0):
        dh_copy(k).start()

    def end_next(j):
        def go(step):
            end_copy(j - 2 * q, step).wait_send()
            end_copy(j, step).start()

        at_ends(go)

    def far_step(j):
        @pl.when(z == 1)
        def _():
            if j == 0:
                end_hp_copy(1).wait_recv()
            end_copy(j, 1).wait_recv()
            for d in range(n_z - 1, 1, -1):
                send_up(d, j, False)

        @pl.when(z == n_z - 2)
        def _():
            if j == 0:
                end_hp_copy(-1).wait_recv()
            end_copy(j, -1).wait_recv()
            for d in range(n_z - 2):
                send_lo(d, j, False)

    def inner_step(j):
        for t in range(n_z - 3):
            @pl.when((z > 1) & (z < n_z - 1 - t))
            def _():
                send_up(n_z - 1 - t, j, True)

            @pl.when((z < n_z - 2) & (z > t))
            def _():
                send_lo(t, j, True)

    def input_grad(pair):
        lo = min(pair) * cap
        for k in pair:
            dh_copy(k).wait_recv()
            d = dh_s[rows(k)].astype(F32) + dh_r[rows(k)].astype(F32)
            route = jnp.sum(d * hid_v[rows(k)], axis=1, keepdims=True)
            route = jnp.broadcast_to(route, (cap, LANES)).astype(BF16)
            a = meta_r[rows(k)].astype(F32)[:, 0:1] * d
            dg[rows(k)] = (a * slope[rows(k)]).astype(BF16)
            du[rows(k)] = (a * act_v[rows(k)]).astype(BF16)
            if k:
                rt_s[rows(k)] = route
                rt_copy(k).start()
            else:
                rt_r[rows(0)] = route
        both = pl.ds(lo, 2 * cap)
        for j in range(nb):
            v = dot(dg[both], wg[cols(j)], 1, 1) + dot(du[both], wu[cols(j)], 1, 1)
            v = v.astype(BF16)
            dx[j, both] = v
            for k in pair:
                if k:
                    back_copy(k, j).start()

    for j in range(q):
        far_step(j)
        end_next(2 * q + j)
    w_in[1].wait()
    w_in[2].wait()
    input_grad((2, 3))
    for j in range(q):
        end_next(3 * q + j)
        inner_step(j)
        far_step(q + j)
    input_grad((1, 0))
    for j in range(2 * q, nb):
        inner_step(j - q)
        far_step(j)
    for j in range(nb - q, nb):
        inner_step(j)

    for j in range(nb):
        v = dot(onehot_t[0, :, :cap], dx[j, rows(0)])
        for k in (1, 2, 3):
            back_copy(k, j).wait_recv()
            v = v + dot(onehot_t[k, :, :cap], back[j, rows(k)])
        tg_ref[:, cols(j)] = v.astype(BF16)
    v0 = jnp.zeros((tokens, LANES), F32)
    v1 = jnp.zeros((tokens, LANES), F32)
    for k in range(4):
        if k:
            rt_copy(k).wait_recv()
        r = dot(onehot_t[k, :, :cap], rt_r[rows(k)])
        v0 = v0 + jnp.where(first == peer[k], r, 0.0)
        v1 = v1 + jnp.where(second == peer[k], r, 0.0)
    pg_ref[...] = jnp.where(row_i == 0, v0.T, v1.T)[:2].astype(BF16)

    own = z
    for j in range(nb):
        hold = dh.at[pl.ds(0, piece), pl.ds(0, bw)]
        hold[...] = product(own, j)

        @pl.when((z == 1) | (z == n_z - 2))
        def _():
            hold[...] += far_product(own, j)

        @pl.when(z > 1)
        def _():
            up_copy(own, j).wait_recv()
            hold[...] += up_r[own, j].astype(F32)

        @pl.when(z < n_z - 2)
        def _():
            lo_copy(own, j).wait_recv()
            hold[...] += lo_r[own, j].astype(F32)

        gd_ref[:, cols(j)] = hold[...].astype(BF16)

    for k in (1, 2, 3):
        meta_copy(k).wait_send()
        rt_copy(k).wait_send()
        for j in range(nb):
            disp_copy(k, j).wait_send()
            back_copy(k, j).wait_send()
    for k in range(4):
        dh_copy(k).wait_send()
    for d in range(n_z):
        for j in range(nb):
            @pl.when((z > 0) & (z < d))
            def _():
                up_copy(d, j).wait_send()

            @pl.when((z < n_z - 1) & (z > d))
            def _():
                lo_copy(d, j).wait_send()

    def ends_sent(step):
        end_hp_copy(step).wait_send()
        for j in range(nb - 2 * q, nb):
            end_copy(j, step).wait_send()

    at_ends(ends_sent)


def fused_shards(n_z, grad_out, route_ids, route_probs, saved_pre, w_gate, w_up, w_down):
    tok, width = grad_out.shape
    slot_rows = saved_pre.shape[2]
    cap = slot_rows // 4
    hidden = saved_pre.shape[3] // 2
    nb = BLOCKS
    bw = width // nb
    piece = hidden // n_z
    vmem = pl.BlockSpec(memory_space=pltpu.VMEM)
    hbm = pl.BlockSpec(memory_space=pl.ANY)
    dma = pltpu.SemaphoreType.DMA
    blocks = (nb, slot_rows, bw)
    hops = (n_z, nb, piece, bw)
    return pl.pallas_call(
        functools.partial(fused, n_z, cap, nb),
        out_shape=(
            jax.ShapeDtypeStruct((tok, width), BF16),
            jax.ShapeDtypeStruct(route_probs.shape[::-1], BF16),
            jax.ShapeDtypeStruct((piece, width), BF16),
        ),
        in_specs=[vmem, vmem, hbm, hbm, hbm, hbm, hbm],
        out_specs=(vmem, vmem, vmem),
        scratch_shapes=[
            pltpu.VMEM((tok, width), BF16),
            pltpu.VMEM((slot_rows, 2 * hidden), BF16),
            pltpu.VMEM((width, hidden), BF16),
            pltpu.VMEM((width, hidden), BF16),
            pltpu.VMEM((hidden, width), BF16),
            pltpu.VMEM((4, tok, LANES), BF16),
            pltpu.VMEM((slot_rows, LANES), BF16),
            pltpu.VMEM((slot_rows, LANES), BF16),
            pltpu.VMEM(blocks, BF16),
            pltpu.VMEM(blocks, BF16),
            pltpu.VMEM((slot_rows, hidden), F32),
            pltpu.VMEM((slot_rows, hidden), F32),
            pltpu.VMEM((slot_rows, hidden), F32),
            pltpu.VMEM((slot_rows, hidden), F32),
            pltpu.VMEM((hidden, slot_rows), BF16),
            pltpu.VMEM((slot_rows, hidden), F32),
            pltpu.VMEM((slot_rows, hidden), BF16),
            pltpu.VMEM((slot_rows, hidden), BF16),
            pltpu.VMEM((slot_rows, hidden), BF16),
            pltpu.VMEM((slot_rows, hidden), BF16),
            pltpu.VMEM(blocks, BF16),
            pltpu.VMEM(blocks, BF16),
            pltpu.VMEM((slot_rows, LANES), BF16),
            pltpu.VMEM((slot_rows, LANES), BF16),
            pltpu.VMEM(hops, BF16),
            pltpu.VMEM(hops, BF16),
            pltpu.VMEM(hops, BF16),
            pltpu.VMEM(hops, BF16),
            pltpu.VMEM(blocks, BF16),
            pltpu.VMEM((hidden, slot_rows), BF16),
            dma((nb,)), dma((4,)), dma((3,)),
            dma((4,)), dma((4,)), dma((4, nb)), dma((4, nb)), dma((4,)), dma((4,)),
            dma((4, nb)), dma((4, nb)), dma((4,)), dma((4,)),
            dma((n_z, nb)), dma((n_z, nb)), dma((n_z, nb)), dma((n_z, nb)), dma((nb + 1,)), dma((nb + 1,)),
        ],
        compiler_params=pltpu.CompilerParams(
            collective_id=0, has_side_effects=True, vmem_limit_bytes=56 * 1024 * 1024
        ),
    )(route_ids.T, route_probs.T, grad_out, saved_pre[0, 0], w_gate[0], w_up[0], w_down[0])


def takes_fused(shape, width, hidden, capacity):
    return (
        shape["expert"] == 4 and shape["tensor"] == 2 and shape["dp"] > 3 and capacity % 16 == 0 and capacity <= LANES
        and width % (BLOCKS * LANES) == 0 and hidden % LANES == 0 and (hidden // shape["dp"]) % 16 == 0
    )


def slot_index(id_block, n_experts, capacity):
    flat = id_block.reshape(-1)
    onehot = (flat[:, None] == jnp.arange(n_experts, dtype=jnp.int32)[None, :]).astype(jnp.int32)
    before = jnp.cumsum(onehot, axis=0) - onehot
    position = jnp.sum(before * onehot, axis=1)
    return flat * capacity + position


def backward_rows(dh_rows, gate, upper, sig, act, hid, p32):
    route = jnp.sum(dh_rows * hid, axis=1).astype(jnp.bfloat16)
    scaled = p32 * dh_rows
    dgate = (scaled * upper * sig * (1.0 + gate * (1.0 - sig))).astype(jnp.bfloat16)
    dup = (scaled * act).astype(jnp.bfloat16)
    return (dgate, dup, route)


def shards(grad_out, route_ids, route_probs, saved_pre, w_gate, w_up, w_down):
    n_exp = lax.axis_size("expert")
    slot_rows = saved_pre.shape[2]
    capacity = slot_rows // n_exp
    tok = grad_out.shape[0]
    topk = route_ids.shape[1]
    width = grad_out.shape[1]
    hidden = saved_pre.shape[3] // 2
    slots = slot_index(route_ids, n_exp, capacity)
    source = (
        jnp.zeros((n_exp * capacity,), jnp.int32)
        .at[slots]
        .set(jnp.arange(tok * topk, dtype=jnp.int32) + 1)
    )
    valid = source > 0
    flat_src = jnp.maximum(source - 1, 0)
    send_rows = jnp.where(valid[:, None], grad_out[flat_src // topk], jnp.zeros((), jnp.bfloat16))
    send_prob = jnp.where(valid, route_probs.reshape(-1)[flat_src], jnp.zeros((), jnp.bfloat16))
    got_rows, got_prob = (
        lax.all_to_all(
            send_rows.reshape(n_exp, capacity, width),
            "expert",
            split_axis=0,
            concat_axis=0,
            tiled=True,
        ),
        lax.all_to_all(
            send_prob.reshape(n_exp, capacity), "expert", split_axis=0, concat_axis=0, tiled=True
        ),
    )
    dyr = got_rows.reshape(slot_rows, width)
    p32 = got_prob.reshape(slot_rows, 1).astype(jnp.float32)
    pre = saved_pre[0, 0]
    gate = pre[:, :hidden].astype(jnp.float32)
    upper = pre[:, hidden:].astype(jnp.float32)
    sig = jax.nn.sigmoid(gate)
    act = gate * sig
    hid = act * upper
    hpro = (p32 * hid).astype(jnp.bfloat16)
    down_term = lax.dot_general(
        hpro, dyr, (((0,), (0,)), ((), ())), preferred_element_type=jnp.float32
    )
    dh_part = lax.dot_general(
        dyr, w_down[0], (((1,), (1,)), ((), ())), preferred_element_type=jnp.float32
    )
    dh_rows = lax.psum(dh_part.astype(jnp.bfloat16), "tensor").astype(jnp.float32)
    dgate, dup, route = backward_rows(dh_rows, gate, upper, sig, act, hid, p32)
    dx = lax.dot_general(
        dgate, w_gate[0], (((1,), (1,)), ((), ())), preferred_element_type=jnp.float32
    )
    dx = dx + lax.dot_general(
        dup, w_up[0], (((1,), (1,)), ((), ())), preferred_element_type=jnp.float32
    )
    dx = dx.astype(jnp.bfloat16)
    back_rows, back_route = (
        lax.all_to_all(
            dx.reshape(n_exp, capacity, width), "expert", split_axis=0, concat_axis=0, tiled=True
        ),
        lax.all_to_all(
            route.reshape(n_exp, capacity), "expert", split_axis=0, concat_axis=0, tiled=True
        ),
    )
    picked = back_rows.reshape(n_exp * capacity, width)[slots].reshape(tok, topk, width)
    token_grad = jnp.sum(picked.astype(jnp.float32), axis=1).astype(jnp.bfloat16)
    prob_grad = back_route.reshape(n_exp * capacity)[slots].reshape(tok, topk)
    grad_down = lax.psum_scatter(
        down_term[None].astype(jnp.bfloat16), "dp", scatter_dimension=1, tiled=True
    )
    return (token_grad, prob_grad, grad_down)


def solution(mesh):
    shape = dict(mesh.shape)

    def local(*args):
        saved_pre, w_down = args[3], args[6]
        capacity = saved_pre.shape[2] // shape["expert"]
        tok = args[0].shape[0]
        if tok == LANES and takes_fused(shape, w_down.shape[2], w_down.shape[1], capacity):
            return tuple(
                v[None] if i == 2 else v.T if i == 1 else v for i, v in enumerate(fused_shards(shape["dp"], *args))
            )
        return shards(*args)

    return jax.shard_map(
        local,
        mesh=mesh,
        in_specs=(
            P(("dp", "expert"), "tensor"),
            P(("dp", "expert"), None),
            P(("dp", "expert"), None),
            P("dp", "expert", None, None),
            P("expert", "tensor", None),
            P("expert", "tensor", None),
            P("expert", None, "tensor"),
        ),
        out_specs=(
            P(("dp", "expert"), "tensor"),
            P(("dp", "expert"), None),
            P("expert", "dp", "tensor"),
        ),
        check_vma=False,
    )
```
